256 devices in a mesh: trial: 16 (over z, core), slab: 8 (over y, x_lo), freq: 2 (over x_hi).
Axes of the slice: x: 4 (x_hi: 2, x_lo: 2; x = x_hi * 2 + x_lo), y: 4, z: 8, core: 2. Of those that a mesh axis runs over, the one named last changes fastest.
Arguments:
- orbitals: float32 [16, 32, 64, 128], P('trial', 'slab'), may hold values from -6 to 6
- energies: float32 [16], P('trial'), may hold values from 0 to 1
- potential: float32 [32, 64, 128], P('slab'), may hold values from 0 to 1
- trials: float32 [128, 32, 64, 128], P('trial', 'slab'), may hold values from -6 to 6
- cheb: float32 [2, 4], P('freq'), may hold values from 0.3 to 1
- shifts: float32 [2], P('freq'), may hold values from -0.5 to 0.5
- column_order: int32 [128], replicated, may hold values from 0 to 127, each once
Outputs:
- gram: float32 [128, 128], P(('trial', 'slab'))
The draws below stay inside these ranges and needn't reach their ends.
Inputs may be any that keep to these rules, and one draw needn't show every extreme that they name: `column_order`: each of 0 to 127 appears once.
All inputs are finite; a program needn't handle non-finite values.
Results may differ from the reference program's by a relative error of at most 0.00024.
Values sent between devices are 32-bit elements; how exact they have to be, the bound alone decides.
No kernel may reach another device: no remote copies, remote signals or barrier semaphores. Data moves between devices by JAX's collectives and lax.ppermute only.
A program may use at most 64 MiB of HBM per device.

```python
import math
import jax
import jax.numpy as jnp
from jax import lax

NY = 64
NZ = 128
KSTEPS = 3
FREQS = 2
TRIALS = 128
NORB = 16
NX = 32


def plane_profile(key, rows):
    phase = jax.random.uniform(key, (rows, 1), jnp.float32, -math.pi, math.pi)
    plane = jnp.arange(NX).astype(jnp.float32)
    profile = 1.0 + 0.3 * jnp.sin(2.0 * math.pi * plane[None] / NX + phase)
    return profile[:, :, None, None]


def draw_orbitals(key, part):
    key_phase = jax.random.fold_in(key, 11)
    key_column = jax.random.fold_in(key, 12)
    key_rough = jax.random.fold_in(key, 13)
    profile = plane_profile(key_phase, NORB)
    column = jnp.clip(jax.random.normal(key_column, (NORB, 1, NY, NZ), jnp.float32), -2.5, 2.5)
    rough = 0.7 * jnp.clip(jax.random.normal(key_rough, (NORB, NX, NY, NZ), jnp.float32), -3.0, 3.0)
    return (profile * column + rough).astype(jnp.float32)


def draw_trials(key, part):
    key_phase = jax.random.fold_in(key, 21)
    key_column = jax.random.fold_in(key, 22)
    key_rough = jax.random.fold_in(key, 23)
    profile = plane_profile(key_phase, TRIALS)
    column = jnp.clip(jax.random.normal(key_column, (TRIALS, 1, NY, NZ), jnp.float32), -2.5, 2.5)
    rough = 0.7 * jnp.clip(jax.random.normal(key_rough, (TRIALS, NX, NY, NZ), jnp.float32), -3.0, 3.0)
    return (profile * column + rough).astype(jnp.float32)


def level_of(key, extent, split, smallest, high):
    factor_of = 1.0
    for position, shards_of in split:
        heights = jax.random.uniform(jax.random.fold_in(jax.random.fold_in(key, 6), position), (shards_of,), jnp.float32, smallest / len(split), high / len(split))
        factor_of = factor_of * jnp.repeat(jnp.exp(heights), extent[position] // shards_of).reshape((-1,) + (1,) * (len(extent) - 1 - position))
    return factor_of


def setup_inputs(seed: int = 0) -> dict:
    key_list = jax.random.split(jax.random.key(seed), 8)
    orbitals = draw_orbitals(jax.random.fold_in(key_list[7], 71), 0)
    energies = jnp.clip(1.0 * jax.random.uniform(key_list[1], (NORB,), jnp.float32) ** level_of(key_list[1], (NORB,), ((0, 16),), -0.2, 0.2), 0.0, 1.0)
    potential = jnp.clip(1.0 * jax.random.uniform(key_list[2], (NX, NY, NZ), jnp.float32) ** level_of(key_list[2], (NX, NY, NZ), ((0, 8),), -0.2, 0.2), 0.0, 1.0)
    trials = draw_trials(jax.random.fold_in(key_list[7], 71), 0)
    cheb = jnp.clip(0.3 + 0.7 * jax.random.uniform(key_list[4], (FREQS, KSTEPS + 1), jnp.float32) ** level_of(key_list[4], (FREQS, KSTEPS + 1), ((0, 2),), -0.2, 0.2), 0.3, 1.0)
    shifts = jnp.clip(jax.random.uniform(key_list[5], (FREQS,), jnp.float32, -0.5, 0.5) * level_of(key_list[5], (FREQS,), ((0, 2),), -0.4, 0.0), -0.5, 0.5)
    column_order = jax.random.permutation(key_list[6], TRIALS).astype(jnp.int32)
    return {"orbitals": orbitals, "energies": energies, "potential": potential, "trials": trials, "cheb": cheb, "shifts": shifts, "column_order": column_order}


def apply_op(field, coef):
    padded = jnp.pad(field, ((0, 0), (1, 1), (1, 1), (1, 1)))
    beside = padded[:, 2:, 1:-1, 1:-1] + padded[:, :-2, 1:-1, 1:-1]
    beside = beside + padded[:, 1:-1, 2:, 1:-1] + padded[:, 1:-1, :-2, 1:-1]
    beside = beside + padded[:, 1:-1, 1:-1, 2:] + padded[:, 1:-1, 1:-1, :-2]
    return (coef[None] * field - 0.5 * beside) / 4.5

def reference(orbitals, energies, potential, trials, cheb, shifts, column_order):
    norb = orbitals.shape[0]

    def one_orbital(carry, item):
        orbital, energy = item
        start = orbital[None] * trials
        parts = []
        for freq in range(FREQS):
            coef = potential - energy - shifts[freq]
            before = start
            now = apply_op(start, coef)
            response = cheb[freq, 0] * start + cheb[freq, 1] * now
            for order in range(2, KSTEPS + 1):
                after = 2.0 * apply_op(now, coef) - before
                response = response + cheb[freq, order] * after
                before, now = (now, after)
            parts.append(orbital[None] * response)
        return (carry + jnp.stack(parts), None)
    empty = jnp.zeros((FREQS, TRIALS, NX, NY, NZ), jnp.float32)
    density, _ = lax.scan(one_orbital, empty, (orbitals, energies))
    total = lax.optimization_barrier(jnp.sum(density, axis=0))
    left = trials.reshape(TRIALS, -1)[column_order]
    right = total.reshape(TRIALS, -1)[column_order]
    gram = jnp.dot(left, right.T, precision=lax.Precision.HIGHEST, preferred_element_type=jnp.float32)
    return gram / jnp.sqrt(jnp.float32(NX * NY * NZ * norb))
```

```python
import functools
import math

import jax
import jax.numpy as jnp
from jax import lax
from jax.experimental import pallas as pl
from jax.experimental.pallas import tpu as pltpu
from jax.sharding import PartitionSpec as P

AXES = ("trial", "slab", "freq")
HOP = 1.0 / 9.0
HIGHEST = lax.Precision.HIGHEST

TILES = ["e", (1, 3), (0, 3), (0, 0), (0, 1), (0, 2), "o", (1, 0), (1, 1), (1, 2)]
ORB_ROW = {(row, plane): row * 4 + plane for row in range(2) for plane in range(4)}
NTILES = len(TILES)


def tile_span(first, last):
    return first * 8, (last + 1) * 8


PARTS = {
    "ahead": (3, 9, 0, 4),
    "above": (1, 6, 2, 0),
    "below": (1, 9, -2, 0),
    "far": (2, 6, 4, 0),
}


def pieces():
    table = {}
    for name, (first, last, drow, dplane) in {"own": (0, 9, 0, 0), **PARTS}.items():
        orb = (TILES.index("o") - first) * 8
        for k in range(first, last + 1):
            tile = TILES[k]
            if isinstance(tile, tuple):
                key = (tile[0] + drow, tile[1] + dplane)
                table[key] = (name, (k - first) * 8, orb + ORB_ROW[tile])
    return table


def pairs():
    own = [(row, plane) for row in range(2) for plane in range(4)]
    ahead = [(row, plane) for row in range(2) for plane in (4, 5, 6)]
    table = {}

    def near(a, b):
        return abs(a[0] - b[0]) + abs(a[1] - b[1]) <= 3

    def add(a, b):
        if near(a, b):
            table.setdefault(a, []).append(b)

    for n, a in enumerate(own):
        table.setdefault(a, []).append(a)
        for b in own[n + 1 :]:
            add(a, b)
        for b in ahead:
            add(a, b)
        for plane in range(4):
            add(a, (2, plane))
        if a[0] == 1:
            for plane in range(4):
                add(a, (-1, plane))
                add(a, (-2, plane))
                add(a, (4, plane))
    for a in ahead:
        if a[0] == 0:
            others = [(-1, plane) for plane in range(4)] + [(2, 3), (-2, 3)]
        else:
            others = [(2, plane) for plane in range(4)] + [(-1, 3), (3, 3)]
        for b in others:
            add(a, b)
    return table


def kernel(place, cheb_ref, v_ref, order_ref, order2_ref, own, ahead, above, below, far, out_ref):
    refs = {"own": own, "ahead": ahead, "above": above, "below": below, "far": far}
    where = pieces()
    lane = lax.broadcasted_iota(jnp.int32, (8, 128), 1)
    slab, block = place[0], place[1]

    energy = own[:, 0, :]
    a0 = a1 = a2 = a3 = jnp.zeros((16, 128), jnp.float32)
    for w in range(2):
        k0, k1, k2, k3, shift = [cheb_ref[w, n : n + 1, :] for n in range(5)]
        c = (energy + shift) / 4.5
        b0, b1, b2, b3 = k0 - k2, k1 - 3.0 * k3, 2.0 * k2, 4.0 * k3
        a3 = a3 + b3
        a2 = a2 + (b2 - 3.0 * c * b3)
        a1 = a1 + (b1 - 2.0 * c * b2 + 3.0 * c * c * b3)
        a0 = a0 + (b0 - c * b1 + c * c * b2 - c * c * c * b3)
    amp = [a0, a1, a2, a3]

    orb = {}

    def orbital(rp):
        if rp not in orb:
            name, _, row = where[rp]
            orb[rp] = refs[name][:, row, :]
        return orb[rp]

    def trial(rp):
        name, row, _ = where[rp]
        return refs[name][:, row : row + 8, :]

    def turn(x, dz):
        return x if dz == 0 else pltpu.roll(x, dz % 128, x.ndim - 1)

    def inside_row(row):
        y = block * 2 + row
        return ((y >= 0) & (y < 64)).astype(jnp.float32)

    def inside_plane(plane):
        x = slab * 4 + plane
        return ((x >= 0) & (x < 32)).astype(jnp.float32)

    def inside_z(dz):
        return ((lane + dz >= 0) & (lane + dz < 128)).astype(jnp.float32)

    pot = {}

    def potential(row, plane):
        if (row, plane) not in pot:
            at = v_ref[plane + 1, row + 1 : row + 2, :] / 4.5
            pot[(row, plane)] = jnp.broadcast_to(at, (8, 128))
        return pot[(row, plane)]

    ones = jnp.ones((8, 128), jnp.float32)

    def powers(a, b, dz):
        dy, dx = b[0] - a[0], b[1] - a[1]
        step = (dx, dy, dz)
        dist = abs(dx) + abs(dy) + abs(dz)
        ways = math.factorial(dist)
        for s in step:
            ways //= math.factorial(abs(s))
        if dist == 3:
            return None, None, None, -(HOP**3) * ways
        vq = potential(*b) if dist < 3 else None
        vp = turn(potential(*a), dz)
        if dist == 2:
            total = float(ways) * (vp + vq)
            moves = [n for n in range(3) if step[n] != 0]
            for n in moves:
                part = [0, 0, 0]
                part[n] = 1 if step[n] > 0 else -1
                mid = potential(a[0] + part[1], a[1] + part[0])
                total = total + turn(mid, dz - part[2])
            return None, None, HOP**2 * ways, HOP**2 * total
        if dist == 1:
            if dz != 0:
                across = inside_row(a[0] - 1) + inside_row(a[0] + 1) + inside_plane(a[1] - 1) + inside_plane(a[1] + 1)
                along = inside_z(-2 * dz) + inside_z(dz)
            else:
                across = inside_z(1) + inside_z(-1)
                if dy != 0:
                    across = across + inside_plane(a[1] - 1) + inside_plane(a[1] + 1)
                    along = inside_row(a[0] - dy) + inside_row(b[0] + dy)
                else:
                    across = across + inside_row(a[0] - 1) + inside_row(a[0] + 1)
                    along = inside_plane(a[1] - dx) + inside_plane(b[1] + dx)
            walks = (3.0 * across + along + 1.0) * ones
            return None, -HOP, -HOP * (vp + vq), -HOP * (vp * vp + vp * vq + vq * vq) - HOP**3 * walks
        around = [(a[0] - 1, a[1]), (a[0] + 1, a[1]), (a[0], a[1] - 1), (a[0], a[1] + 1)]
        degree = inside_z(1) + inside_z(-1)
        near = inside_z(-1) * turn(vp, 1) + inside_z(1) * turn(vp, -1)
        for row, plane in around:
            here = inside_row(row) * inside_plane(plane)
            degree = degree + here
            near = near + here * potential(row, plane)
        square = vp * vp
        return 1.0, vp, square + HOP**2 * degree, vp * square + HOP**2 * (2.0 * degree * vp + near)

    def coefficient(a, b, dz, left):
        right = orbital(b)
        total = None
        for m, h in enumerate(powers(a, b, dz)):
            if h is None:
                continue
            product = left[m] * right
            term = (product[:8] + product[8:]) * h
            total = term if total is None else total + term
        for s in (4, 2, 1):
            total = total + pltpu.roll(total, s, 0)
        if a == b and dz == 0:
            total = total * 0.5
        if dz != 0:
            total = total * inside_z(-dz)
        return total

    gram = jnp.zeros((128, 128), jnp.float32)
    for a, rights in pairs().items():
        response = None
        for dz in range(-3, 4):
            todo = []
            for b in rights:
                dist = abs(a[0] - b[0]) + abs(a[1] - b[1]) + abs(dz)
                if dist <= 3 and (a != b or dz >= 0):
                    todo.append((b, dist))
            if not todo:
                continue
            moved = turn(orbital(a), dz)
            least = min(dist for _, dist in todo)
            left = [moved * amp[m] if m >= least else None for m in range(4)]
            acc = None
            for b, _ in todo:
                term = coefficient(a, b, dz, left)[None] * trial(b)
                acc = term if acc is None else acc + term
            acc = turn(acc.reshape(128, 128), -dz)
            response = acc if response is None else response + acc
        gram = gram + lax.dot_general(
            trial(a).reshape(128, 128), response, (((1,), (1,)), ((), ())),
            precision=HIGHEST, preferred_element_type=jnp.float32,
        )

    gram = (gram + gram.T) * (1.0 / math.sqrt(32 * 64 * 128 * 16))
    pick = (order_ref[...] == lax.broadcasted_iota(jnp.int32, (128, 128), 0)).astype(jnp.float32)
    pick2 = (order2_ref[...] == lax.broadcasted_iota(jnp.int32, (128, 256), 0)).astype(jnp.float32)
    gram = jnp.dot(gram, pick, precision=HIGHEST, preferred_element_type=jnp.float32)
    out_ref[...] = lax.dot_general(
        pick2, gram, (((0,), (0,)), ((), ())), precision=HIGHEST, preferred_element_type=jnp.float32
    )


def shift_perm(step, dslab):
    perm = []
    for trial in range(16):
        for slab in range(8):
            for freq in range(2):
                block = freq * 16 + trial + step
                other = slab + dslab
                if 0 <= block < 32 and 0 <= other < 8:
                    source = ((block % 16) * 8 + other) * 2 + block // 16
                    perm.append((source, (trial * 8 + slab) * 2 + freq))
    return perm


def local(orbitals, energies, potential, trials, cheb, shifts, column_order):
    trial, slab, freq = (lax.axis_index(a) for a in AXES)
    block = freq * 16 + trial

    padded = jnp.pad(potential, ((0, 0), (1, 7), (0, 0)))
    window = lax.dynamic_slice_in_dim(padded, block * 2, 8, axis=1)
    scalars = jnp.concatenate([cheb[0], shifts, jnp.zeros((3,), jnp.float32)])
    scalars = jnp.broadcast_to(scalars[:, None], (8, 128))
    swap = [
        ((t * 8 + (s + 1) % 8) * 2 + 1 - f, (t * 8 + s) * 2 + f)
        for t in range(16) for s in range(8) for f in range(2)
    ]
    other = lax.dynamic_slice_in_dim(padded, (block ^ 16) * 2, 8, axis=1)
    up = lax.ppermute(jnp.concatenate([other[:2], scalars[None]]), AXES, swap)
    down = lax.ppermute(window[3:4], "slab", [(s, s + 1) for s in range(7)])
    v = jnp.concatenate([down, window, up[:2]])
    both = jnp.stack([scalars, up[2]])

    rows = lax.dynamic_slice_in_dim(trials, freq * 32, 32, axis=2)
    rows = rows.reshape(8, 4, 16, 2, 128).transpose(2, 3, 1, 0, 4)
    orb = lax.dynamic_slice_in_dim(orbitals, freq * 32, 32, axis=2)
    orb = orb.reshape(4, 16, 2, 128).transpose(1, 2, 0, 3).reshape(16, 8, 128)
    energy = jnp.broadcast_to(energies.reshape(1, 1, 1), (16, 8, 128))
    send = [
        energy if t == "e" else orb if t == "o" else rows[:, t[0], t[1]] for t in TILES
    ]
    own = lax.all_to_all(jnp.concatenate(send, axis=1), "trial", split_axis=0, concat_axis=0, tiled=True)

    steps = {"ahead": (0, 1), "above": (1, 0), "below": (-1, 0), "far": (2, 0)}
    halo = {}
    for name, (first, last, _, _) in PARTS.items():
        start, stop = tile_span(first, last)
        halo[name] = lax.ppermute(own[:, start:stop], AXES, shift_perm(*steps[name]))

    place = jnp.stack([slab, block]).astype(jnp.int32)
    smem = pl.BlockSpec(memory_space=pltpu.SMEM)
    vmem = pl.BlockSpec(memory_space=pltpu.VMEM)
    partial = pl.pallas_call(
        kernel,
        out_shape=jax.ShapeDtypeStruct((256, 128), jnp.float32),
        in_specs=[smem] + [vmem] * 9,
        out_specs=vmem,
        compiler_params=pltpu.CompilerParams(vmem_limit_bytes=32 * 1024 * 1024),
    )(
        place, both, v, column_order[None], jnp.repeat(column_order, 2)[None],
        own, halo["ahead"], halo["above"], halo["below"], halo["far"],
    )
    terms = lax.all_to_all(partial, AXES, split_axis=0, concat_axis=0, tiled=True)
    return jnp.sum(terms, axis=0, keepdims=True)


def solution(mesh):
    in_specs = (
        P("trial", "slab", None, None),
        P("trial"),
        P("slab", None, None),
        P("trial", "slab", None, None),
        P("freq", None),
        P("freq"),
        P(),
    )
    out_specs = P(("trial", "slab"), None)
    return jax.shard_map(local, mesh=mesh, in_specs=in_specs, out_specs=out_specs, check_vma=False)
```

```python
import math

import jax
import jax.numpy as jnp
from jax import lax
from jax.experimental import pallas as pl
from jax.experimental.pallas import tpu as pltpu
from jax.sharding import PartitionSpec as P

AXES = ("trial", "slab", "freq")
HOP = 1.0 / 9.0
HIGHEST = lax.Precision.HIGHEST

TILES = [(1, 3), (0, 3), (0, 0), (0, 1), (0, 2), "o", (1, 0), (1, 1), (1, 2), "e"]
ORB = TILES.index("o") * 8
EXTRA = TILES.index("e") * 8
OWN = [(row, plane) for row in range(2) for plane in range(4)]
AHEAD = [(row, plane) for row in range(2) for plane in range(3)]


def pieces():
    table = {}
    for k, tile in enumerate(TILES):
        if isinstance(tile, tuple):
            row, plane = tile
            orb = ORB + row * 4 + plane
            table[tile] = ("own", k * 8, orb)
            table[(row - 2, plane)] = ("below", k * 8, orb)
            if k < 6:
                table[(row + 2, plane)] = ("above", k * 8, orb)
    for k, (row, plane) in enumerate(AHEAD):
        table[(row, plane + 4)] = ("ahead", k * 8, 48 + k)
    return table


def pairs():
    ahead = [(row, plane + 4) for row, plane in AHEAD]
    table = {}

    def near(a, b):
        return abs(a[0] - b[0]) + abs(a[1] - b[1]) <= 3

    def add(a, b):
        if near(a, b):
            table.setdefault(a, []).append(b)

    for n, a in enumerate(OWN):
        table.setdefault(a, []).append(a)
        for b in OWN[n + 1 :]:
            add(a, b)
        for b in ahead:
            add(a, b)
        for plane in range(4):
            add(a, (2, plane))
        if a[0] == 1:
            for plane in range(4):
                add(a, (-1, plane))
                add(a, (-2, plane))
    for a in ahead:
        if a[1] == 4:
            add(a, a)
        if a[0] == 0:
            others = [(-1, plane) for plane in range(4)] + [(2, 3), (-2, 3)]
        else:
            others = [(2, plane) for plane in range(4)] + [(-1, 3), (3, 3)]
        for b in others:
            add(a, b)
    for plane in range(4):
        add((-1, plane), (2, plane))
    return table


def pack_kernel(energy, cheb, shift, trials_hbm, orbital_hbm, potential_hbm, out_ref, trials, orbital, potential, sems):
    trial, slab, freq = (lax.axis_index(a) for a in AXES)
    half = freq ^ (slab & 1)
    rows = pl.ds(pl.multiple_of(half * 32, 32), 32)
    copies = [
        pltpu.make_async_copy(source, target, sems.at[n])
        for n, (source, target) in enumerate(
            [
                (trials_hbm.at[:, rows, :], trials.reshape(32, 32, 128)),
                (orbital_hbm.at[:, rows, :], orbital.reshape(4, 32, 128)),
                (potential_hbm, potential.reshape(4, 64, 128)),
            ]
        )
    ]
    for copy in copies:
        copy.start()
    row_of = lax.broadcasted_iota(jnp.int32, (8, 128), 0)
    lane = lax.broadcasted_iota(jnp.int32, (8, 128), 1)
    scalars = jnp.where(row_of == 0, energy[0], 0.0)
    for n, value in enumerate([cheb[0, 0], cheb[0, 1], cheb[0, 2], cheb[0, 3], shift[0]]):
        scalars = jnp.where((row_of == n + 2) | ((row_of == 7) & (lane == n)), value, scalars)
    for copy in copies:
        copy.wait()
    for t in range(16):
        for k, tile in enumerate(TILES):
            if tile == "o":
                for row in range(2):
                    out_ref[t, k * 8 + 4 * row : k * 8 + 4 * row + 4, :] = orbital[pl.ds(2 * t + row, 4, stride=32), :]
            elif tile == "e":
                y = jnp.clip(half * 32 + 2 * t + lax.rem(trial, 4) - 1, 0, 63)
                at = potential[pl.ds(lax.div(trial, 4) * 64 + y, 1), :]
                out_ref[t, k * 8 : k * 8 + 8, :] = jnp.where(row_of == 1, at, scalars)
            else:
                out_ref[t, k * 8 : k * 8 + 8, :] = trials[pl.ds(tile[1] * 32 + 2 * t + tile[0], 8, stride=128), :]


def halo_kernel(own, ahead, above):
    for k, (row, plane) in enumerate(AHEAD):
        start = TILES.index((row, plane)) * 8
        ahead[:, k * 8 : k * 8 + 8, :] = own[:, start : start + 8, :]
        orb = ORB + row * 4 + plane
        ahead[:, 48 + k : 49 + k, :] = own[:, orb : orb + 1, :]
    ahead[:, 54:55, :] = own[:, EXTRA + 1 : EXTRA + 2, :]
    ahead[:, 55:56, :] = own[:, EXTRA + 7 : EXTRA + 8, :]
    above[...] = own[:, :48, :]


def kernel(order_ref, order2_ref, own, ahead, above, below, out_ref):
    refs = {"own": own, "ahead": ahead, "above": above, "below": below}
    where = pieces()
    lane = lax.broadcasted_iota(jnp.int32, (8, 128), 1)
    trial_index, slab, freq = (lax.axis_index(a) for a in AXES)
    block = (freq ^ (slab & 1)) * 16 + trial_index

    energy = own[:, EXTRA, :]
    theirs = ahead[0, 55:56, :]
    a0 = a1 = a2 = a3 = jnp.zeros((16, 128), jnp.float32)
    for scalars in (
        [own[0, EXTRA + n : EXTRA + n + 1, :] for n in range(2, 7)],
        [jnp.broadcast_to(theirs[:, n : n + 1], (1, 128)) for n in range(5)],
    ):
        k0, k1, k2, k3, shift = scalars
        c = (energy + shift) / 4.5
        b0, b1, b2, b3 = k0 - k2, k1 - 3.0 * k3, 2.0 * k2, 4.0 * k3
        a3 = a3 + b3
        a2 = a2 + (b2 - 3.0 * c * b3)
        a1 = a1 + (b1 - 2.0 * c * b2 + 3.0 * c * c * b3)
        a0 = a0 + (b0 - c * b1 + c * c * b2 - c * c * c * b3)
    amp = [a0, a1, a2, a3]

    orb = {}

    def orbital(rp):
        if rp not in orb:
            name, _, row = where[rp]
            orb[rp] = refs[name][:, row, :]
            if name == "ahead":
                orb[rp] = orb[rp] * inside_plane(4)
        return orb[rp]

    def trial(rp):
        name, row, _ = where[rp]
        return refs[name][:, row : row + 8, :]

    def turn(x, dz):
        return x if dz == 0 else pltpu.roll(x, dz % 128, x.ndim - 1)

    def inside_row(row):
        y = block * 2 + row
        return ((y >= 0) & (y < 64)).astype(jnp.float32)

    def inside_plane(plane):
        x = slab * 4 + plane
        return ((x >= 0) & (x < 32)).astype(jnp.float32)

    def inside_z(dz):
        return ((lane + dz >= 0) & (lane + dz < 128)).astype(jnp.float32)

    pot = {}

    def potential(row, plane):
        if (row, plane) not in pot:
            ref, at = (own, EXTRA + 1) if plane < 4 else (ahead, 54)
            source = plane % 4 * 4 + row + 1
            pot[(row, plane)] = jnp.broadcast_to(ref[source, at : at + 1, :] / 4.5, (8, 128))
        return pot[(row, plane)]

    ones = jnp.ones((8, 128), jnp.float32)

    def powers(a, b, dz):
        dy, dx = b[0] - a[0], b[1] - a[1]
        step = (dx, dy, dz)
        dist = abs(dx) + abs(dy) + abs(dz)
        ways = math.factorial(dist)
        for s in step:
            ways //= math.factorial(abs(s))
        if dist == 3:
            return None, None, None, -(HOP**3) * ways
        vq = potential(*b) if dist < 3 else None
        vp = turn(potential(*a), dz)
        if dist == 2:
            total = float(ways) * (vp + vq)
            moves = [n for n in range(3) if step[n] != 0]
            for n in moves:
                part = [0, 0, 0]
                part[n] = 1 if step[n] > 0 else -1
                mid = potential(a[0] + part[1], a[1] + part[0])
                total = total + turn(mid, dz - part[2])
            return None, None, HOP**2 * ways, HOP**2 * total
        if dist == 1:
            if dz != 0:
                across = inside_row(a[0] - 1) + inside_row(a[0] + 1) + inside_plane(a[1] - 1) + inside_plane(a[1] + 1)
                along = inside_z(-2 * dz) + inside_z(dz)
            else:
                across = inside_z(1) + inside_z(-1)
                if dy != 0:
                    across = across + inside_plane(a[1] - 1) + inside_plane(a[1] + 1)
                    along = inside_row(a[0] - dy) + inside_row(b[0] + dy)
                else:
                    across = across + inside_row(a[0] - 1) + inside_row(a[0] + 1)
                    along = inside_plane(a[1] - dx) + inside_plane(b[1] + dx)
            walks = (3.0 * across + along + 1.0) * ones
            return None, -HOP, -HOP * (vp + vq), -HOP * (vp * vp + vp * vq + vq * vq) - HOP**3 * walks
        if a[1] == 4:
            return None, None, None, HOP**2 * potential(a[0], 3)
        around = [(a[0] - 1, a[1]), (a[0] + 1, a[1]), (a[0], a[1] - 1), (a[0], a[1] + 1)]
        degree = inside_z(1) + inside_z(-1)
        near = inside_z(-1) * turn(vp, 1) + inside_z(1) * turn(vp, -1)
        for row, plane in around:
            here = inside_row(row) * inside_plane(plane)
            degree = degree + here
            if plane >= 0:
                near = near + here * potential(row, plane)
        square = vp * vp
        return 1.0, vp, square + HOP**2 * degree, vp * square + HOP**2 * (2.0 * degree * vp + near)

    def coefficient(a, b, dz, left):
        right = orbital(b)
        total = None
        for m, h in enumerate(powers(a, b, dz)):
            if h is None:
                continue
            product = left[m] * right
            term = (product[:8] + product[8:]) * h
            total = term if total is None else total + term
        for s in (4, 2, 1):
            total = total + pltpu.roll(total, s, 0)
        if a == b and dz == 0:
            total = total * 0.5
        if dz != 0:
            total = total * inside_z(-dz)
        return total

    gram = jnp.zeros((128, 128), jnp.float32)
    for a, rights in pairs().items():
        response = None
        for dz in range(-3, 4):
            todo = []
            for b in rights:
                dist = abs(a[0] - b[0]) + abs(a[1] - b[1]) + abs(dz)
                if dist <= 3 and (a != b or dz == 0 or (dz > 0 and a[1] < 4)):
                    todo.append((b, dist))
            if not todo:
                continue
            moved = turn(orbital(a), dz)
            least = min(dist for _, dist in todo)
            left = [moved * amp[m] if m >= least else None for m in range(4)]
            acc = None
            for b, _ in todo:
                term = coefficient(a, b, dz, left)[None] * trial(b)
                acc = term if acc is None else acc + term
            acc = turn(acc.reshape(128, 128), -dz)
            response = acc if response is None else response + acc
        gram = gram + lax.dot_general(
            trial(a).reshape(128, 128), response, (((1,), (1,)), ((), ())),
            precision=HIGHEST, preferred_element_type=jnp.float32,
        )

    gram = (gram + gram.T) * (1.0 / math.sqrt(32 * 64 * 128 * 16))
    pick = (order_ref[...] == lax.broadcasted_iota(jnp.int32, (128, 128), 0)).astype(jnp.float32)
    pick2 = (order2_ref[...] == lax.broadcasted_iota(jnp.int32, (128, 256), 0)).astype(jnp.float32)
    gram = jnp.dot(gram, pick, precision=HIGHEST, preferred_element_type=jnp.float32)
    out_ref[...] = lax.dot_general(
        pick2, gram, (((0,), (0,)), ((), ())), precision=HIGHEST, preferred_element_type=jnp.float32
    )


def device(block, slab):
    return ((block % 16) * 8 + slab) * 2 + ((block // 16) ^ (slab & 1))


def shift_perm(step, dslab):
    return [
        (device(block + step, (slab + dslab) % 8), device(block, slab))
        for block in range(32)
        for slab in range(8)
        if 0 <= block + step < 32
    ]


def local(orbitals, energies, potential, trials, cheb, shifts, column_order):
    smem = pl.BlockSpec(memory_space=pltpu.SMEM)
    vmem = pl.BlockSpec(memory_space=pltpu.VMEM)
    params = pltpu.CompilerParams(vmem_limit_bytes=32 * 1024 * 1024)

    def shape(rows, lead=(16,)):
        return jax.ShapeDtypeStruct((*lead, rows, 128), jnp.float32)

    send = pl.pallas_call(
        pack_kernel,
        out_shape=shape(len(TILES) * 8),
        in_specs=[smem] * 3 + [pl.BlockSpec(memory_space=pltpu.HBM)] * 3,
        out_specs=vmem,
        scratch_shapes=[
            pltpu.VMEM((1024, 128), jnp.float32),
            pltpu.VMEM((128, 128), jnp.float32),
            pltpu.VMEM((256, 128), jnp.float32),
            pltpu.SemaphoreType.DMA((3,)),
        ],
        compiler_params=pltpu.CompilerParams(vmem_limit_bytes=60 * 1024 * 1024),
    )(energies, cheb, shifts, trials.reshape(32, 64, 128), orbitals[0], potential)
    own = lax.all_to_all(send, "trial", split_axis=0, concat_axis=0, tiled=True)

    ahead, above = pl.pallas_call(
        halo_kernel,
        out_shape=[shape(56), shape(48)],
        in_specs=[vmem],
        out_specs=[vmem] * 2,
        compiler_params=params,
    )(own)
    ahead = lax.ppermute(ahead, AXES, shift_perm(0, 1))
    below = lax.ppermute(own, AXES, shift_perm(-1, 0))
    above = lax.ppermute(above, AXES, shift_perm(1, 0))

    partial = pl.pallas_call(
        kernel,
        out_shape=shape(256, ()),
        in_specs=[vmem] * 6,
        out_specs=vmem,
        compiler_params=params,
    )(column_order[None], jnp.repeat(column_order, 2)[None], own, ahead, above, below)
    terms = lax.all_to_all(partial, AXES, split_axis=0, concat_axis=0, tiled=True)
    return jnp.sum(terms, axis=0, keepdims=True)


def solution(mesh):
    in_specs = (
        P("trial", "slab", None, None),
        P("trial"),
        P("slab", None, None),
        P("trial", "slab", None, None),
        P("freq", None),
        P("freq"),
        P(),
    )
    out_specs = P(("trial", "slab"), None)
    return jax.shard_map(local, mesh=mesh, in_specs=in_specs, out_specs=out_specs, check_vma=False)
```

```python
import math

import jax
import jax.numpy as jnp
from jax import lax
from jax.experimental import pallas as pl
from jax.experimental.pallas import tpu as pltpu
from jax.sharding import PartitionSpec as P

AXES = ("trial", "slab", "freq")
HOP = 1.0 / 9.0
HIGHEST = lax.Precision.HIGHEST

TILES = [(0, 0), (0, 1), (0, 2), (0, 3), (1, 0), (1, 1), (1, 2), (1, 3), "o", "e"]
ORB = TILES.index("o") * 8
EXTRA = TILES.index("e") * 8
OWN = [(row, plane) for row in range(2) for plane in range(4)]
PARTS = {
    "ahead": ([(row, plane) for row in range(2) for plane in range(3)], 0, 4),
    "above": ([(0, 0), (0, 1), (0, 2), (0, 3), (1, 0), (1, 1), (1, 3)], 2, 0),
    "below": ([(1, 0), (1, 1), (1, 2), (1, 3), (0, 2), (0, 3)], -2, 0),
}
AHEAD = PARTS["ahead"][0]


def pieces():
    table = {}
    for rp in OWN:
        table[rp] = ("own", TILES.index(rp) * 8, ORB + OWN.index(rp))
    for name, (taken, drow, dplane) in PARTS.items():
        for k, rp in enumerate(taken):
            orb = k if name == "ahead" else OWN.index(rp)
            table[(rp[0] + drow, rp[1] + dplane)] = (name, k * 8, len(taken) * 8 + orb)
    return table


def pairs():
    ahead = [(row, plane + 4) for row, plane in AHEAD]
    table = {}

    def near(a, b):
        return abs(a[0] - b[0]) + abs(a[1] - b[1]) <= 3

    def add(a, b):
        if near(a, b):
            table.setdefault(a, []).append(b)

    for n, a in enumerate(OWN):
        table.setdefault(a, []).append(a)
        for b in OWN[n + 1 :]:
            add(a, b)
        for b in ahead:
            add(a, b)
        for plane in range(4):
            add(a, (2, plane))
        if a[0] == 1:
            for plane in range(4):
                add(a, (-1, plane))
        if a in ((0, 0), (0, 1), (0, 3)):
            add(a, (3, a[1]))
        if a == (1, 2):
            add(a, (-2, 2))
    for a in ahead:
        if a[1] == 4:
            add(a, a)
        if a[0] == 0:
            others = [(-1, plane) for plane in range(4)] + [(2, 3), (-2, 3)]
        else:
            others = [(2, plane) for plane in range(4)] + [(-1, 3), (3, 3)]
        for b in others:
            add(a, b)
    for plane in range(4):
        add((-1, plane), (2, plane))
    return table


def half_of(slab, freq):
    return freq ^ (((slab + 1) // 2) & 1)


def pack_kernel(energy, cheb, shift, trials_hbm, orbital_hbm, potential_hbm, out_ref, scalars_ref, trials, orbital, potential, sems):
    trial, slab, freq = (lax.axis_index(a) for a in AXES)
    half = freq ^ (lax.div(slab + 1, 2) & 1)
    rows = pl.ds(pl.multiple_of(half * 32, 32), 32)
    copies = [
        pltpu.make_async_copy(source, target, sems.at[n])
        for n, (source, target) in enumerate(
            [
                (trials_hbm.at[:, rows, :], trials.reshape(32, 32, 128)),
                (orbital_hbm.at[:, rows, :], orbital.reshape(4, 32, 128)),
                (potential_hbm, potential.reshape(4, 64, 128)),
            ]
        )
    ]
    for copy in copies:
        copy.start()
    row_of = lax.broadcasted_iota(jnp.int32, (8, 128), 0)
    scalars = jnp.where(row_of == 0, energy[0], 0.0)
    for n, value in enumerate([cheb[0, 0], cheb[0, 1], cheb[0, 2], cheb[0, 3], shift[0]]):
        scalars = jnp.where(row_of == n + 2, value, scalars)
    scalars_ref[...] = scalars
    for copy in copies:
        copy.wait()
    for t in range(16):
        for k, tile in enumerate(TILES):
            if tile == "o":
                for row in range(2):
                    out_ref[t, k * 8 + 4 * row : k * 8 + 4 * row + 4, :] = orbital[pl.ds(2 * t + row, 4, stride=32), :]
            elif tile == "e":
                y = jnp.clip(half * 32 + 2 * t + lax.rem(trial, 4) - 1, 0, 63)
                at = potential[pl.ds(lax.div(trial, 4) * 64 + y, 1), :]
                out_ref[t, k * 8 : k * 8 + 8, :] = jnp.where(row_of == 1, at, scalars)
            else:
                out_ref[t, k * 8 : k * 8 + 8, :] = trials[pl.ds(tile[1] * 32 + 2 * t + tile[0], 8, stride=128), :]


def halo_kernel(own, theirs, ahead, above, below, theirs_ref):
    theirs_ref[...] = theirs[...]
    for name, ref in (("ahead", ahead), ("above", above), ("below", below)):
        taken = PARTS[name][0]
        for k, rp in enumerate(taken):
            start = TILES.index(rp) * 8
            ref[:, k * 8 : k * 8 + 8, :] = own[:, start : start + 8, :]
        if name != "ahead":
            ref[:, len(taken) * 8 :, :] = own[:, ORB : ORB + 8, :]
    last = [ORB + OWN.index(rp) for rp in AHEAD] + [EXTRA + 1, EXTRA + 1]
    for k, row in enumerate(last):
        ahead[:, 48 + k : 49 + k, :] = own[:, row : row + 1, :]


def kernel(order_ref, order2_ref, theirs, own, ahead, above, below, out_ref):
    refs = {"own": own, "ahead": ahead, "above": above, "below": below}
    where = pieces()
    lane = lax.broadcasted_iota(jnp.int32, (8, 128), 1)
    trial_index, slab, freq = (lax.axis_index(a) for a in AXES)
    block = (freq ^ (lax.div(slab + 1, 2) & 1)) * 16 + trial_index

    energy = own[:, EXTRA, :]
    a0 = a1 = a2 = a3 = jnp.zeros((16, 128), jnp.float32)
    for ref, first in ((own.at[0], EXTRA + 2), (theirs, 2)):
        k0, k1, k2, k3, shift = [ref[first + n : first + n + 1, :] for n in range(5)]
        c = (energy + shift) / 4.5
        b0, b1, b2, b3 = k0 - k2, k1 - 3.0 * k3, 2.0 * k2, 4.0 * k3
        a3 = a3 + b3
        a2 = a2 + (b2 - 3.0 * c * b3)
        a1 = a1 + (b1 - 2.0 * c * b2 + 3.0 * c * c * b3)
        a0 = a0 + (b0 - c * b1 + c * c * b2 - c * c * c * b3)
    amp = [a0, a1, a2, a3]

    orb = {}

    def orbital(rp):
        if rp not in orb:
            name, _, row = where[rp]
            orb[rp] = refs[name][:, row, :]
        return orb[rp]

    def trial(rp):
        name, row, _ = where[rp]
        return refs[name][:, row : row + 8, :]

    def turn(x, dz):
        return x if dz == 0 else pltpu.roll(x, dz % 128, x.ndim - 1)

    def inside_row(row):
        y = block * 2 + row
        return ((y >= 0) & (y < 64)).astype(jnp.float32)

    def inside_plane(plane):
        x = slab * 4 + plane
        return ((x >= 0) & (x < 32)).astype(jnp.float32)

    def inside_z(dz):
        return ((lane + dz >= 0) & (lane + dz < 128)).astype(jnp.float32)

    pot = {}

    def potential(row, plane):
        if (row, plane) not in pot:
            ref, at = (own, EXTRA + 1) if plane < 4 else (ahead, 54)
            source = plane % 4 * 4 + row + 1
            pot[(row, plane)] = jnp.broadcast_to(ref[source, at : at + 1, :] / 4.5, (8, 128))
        return pot[(row, plane)]

    ones = jnp.ones((8, 128), jnp.float32)

    def powers(a, b, dz):
        dy, dx = b[0] - a[0], b[1] - a[1]
        step = (dx, dy, dz)
        dist = abs(dx) + abs(dy) + abs(dz)
        ways = math.factorial(dist)
        for s in step:
            ways //= math.factorial(abs(s))
        if dist == 3:
            return None, None, None, -(HOP**3) * ways
        vq = potential(*b) if dist < 3 else None
        vp = turn(potential(*a), dz)
        if dist == 2:
            total = float(ways) * (vp + vq)
            moves = [n for n in range(3) if step[n] != 0]
            for n in moves:
                part = [0, 0, 0]
                part[n] = 1 if step[n] > 0 else -1
                mid = potential(a[0] + part[1], a[1] + part[0])
                total = total + turn(mid, dz - part[2])
            return None, None, HOP**2 * ways, HOP**2 * total
        if dist == 1:
            if dz != 0:
                across = inside_row(a[0] - 1) + inside_row(a[0] + 1) + inside_plane(a[1] - 1) + inside_plane(a[1] + 1)
                along = inside_z(-2 * dz) + inside_z(dz)
            else:
                across = inside_z(1) + inside_z(-1)
                if dy != 0:
                    across = across + inside_plane(a[1] - 1) + inside_plane(a[1] + 1)
                    along = inside_row(a[0] - dy) + inside_row(b[0] + dy)
                else:
                    across = across + inside_row(a[0] - 1) + inside_row(a[0] + 1)
                    along = inside_plane(a[1] - dx) + inside_plane(b[1] + dx)
            walks = (3.0 * across + along + 1.0) * ones
            return None, -HOP, -HOP * (vp + vq), -HOP * (vp * vp + vp * vq + vq * vq) - HOP**3 * walks
        if a[1] == 4:
            return None, None, None, HOP**2 * potential(a[0], 3)
        around = [(a[0] - 1, a[1]), (a[0] + 1, a[1]), (a[0], a[1] - 1), (a[0], a[1] + 1)]
        degree = inside_z(1) + inside_z(-1)
        near = inside_z(-1) * turn(vp, 1) + inside_z(1) * turn(vp, -1)
        for row, plane in around:
            here = inside_row(row) * inside_plane(plane)
            degree = degree + here
            if plane >= 0:
                near = near + here * potential(row, plane)
        square = vp * vp
        return 1.0, vp, square + HOP**2 * degree, vp * square + HOP**2 * (2.0 * degree * vp + near)

    def coefficient(a, b, dz, left):
        right = orbital(b)
        total = None
        for m, h in enumerate(powers(a, b, dz)):
            if h is None:
                continue
            product = left[m] * right
            term = (product[:8] + product[8:]) * h
            total = term if total is None else total + term
        for s in (4, 2, 1):
            total = total + pltpu.roll(total, s, 0)
        if a == b and dz == 0:
            total = total * 0.5
        if dz != 0:
            total = total * inside_z(-dz)
        return total

    gram = jnp.zeros((128, 128), jnp.float32)
    for a, rights in pairs().items():
        response = None
        for dz in range(-3, 4):
            todo = []
            for b in rights:
                dist = abs(a[0] - b[0]) + abs(a[1] - b[1]) + abs(dz)
                if dist <= 3 and (a != b or dz == 0 or (dz > 0 and a[1] < 4)):
                    todo.append((b, dist))
            if not todo:
                continue
            moved = turn(orbital(a), dz)
            least = min(dist for _, dist in todo)
            left = [moved * amp[m] if m >= least else None for m in range(4)]
            acc = None
            for b, _ in todo:
                term = coefficient(a, b, dz, left)[None] * trial(b)
                acc = term if acc is None else acc + term
            acc = turn(acc.reshape(128, 128), -dz)
            response = acc if response is None else response + acc
        gram = gram + lax.dot_general(
            trial(a).reshape(128, 128), response, (((1,), (1,)), ((), ())),
            precision=HIGHEST, preferred_element_type=jnp.float32,
        )

    gram = (gram + gram.T) * (1.0 / math.sqrt(32 * 64 * 128 * 16))
    pick = (order_ref[...] == lax.broadcasted_iota(jnp.int32, (128, 128), 0)).astype(jnp.float32)
    pick2 = (order2_ref[...] == lax.broadcasted_iota(jnp.int32, (128, 256), 0)).astype(jnp.float32)
    gram = jnp.dot(gram, pick, precision=HIGHEST, preferred_element_type=jnp.float32)
    out_ref[...] = lax.dot_general(
        pick2, gram, (((0,), (0,)), ((), ())), precision=HIGHEST, preferred_element_type=jnp.float32
    )


def device(block, slab):
    return ((block % 16) * 8 + slab) * 2 + half_of(slab, block // 16)


def shift_perm(step, dslab):
    return [
        (device(block + step, slab + dslab), device(block, slab))
        for block in range(32)
        for slab in range(8)
        if 0 <= block + step < 32 and slab + dslab < 8
    ]


def local(orbitals, energies, potential, trials, cheb, shifts, column_order):
    smem = pl.BlockSpec(memory_space=pltpu.SMEM)
    vmem = pl.BlockSpec(memory_space=pltpu.VMEM)
    params = pltpu.CompilerParams(vmem_limit_bytes=32 * 1024 * 1024)

    def shape(rows, lead=(16,)):
        return jax.ShapeDtypeStruct((*lead, rows, 128), jnp.float32)

    send, scalars = pl.pallas_call(
        pack_kernel,
        out_shape=[shape(len(TILES) * 8), shape(8, ())],
        in_specs=[smem] * 3 + [pl.BlockSpec(memory_space=pltpu.HBM)] * 3,
        out_specs=[vmem] * 2,
        scratch_shapes=[
            pltpu.VMEM((1024, 128), jnp.float32),
            pltpu.VMEM((128, 128), jnp.float32),
            pltpu.VMEM((256, 128), jnp.float32),
            pltpu.SemaphoreType.DMA((3,)),
        ],
        compiler_params=pltpu.CompilerParams(vmem_limit_bytes=60 * 1024 * 1024),
    )(energies, cheb, shifts, trials.reshape(32, 64, 128), orbitals[0], potential)
    own = lax.all_to_all(send, "trial", split_axis=0, concat_axis=0, tiled=True)

    theirs = lax.ppermute(scalars, "freq", [(0, 1), (1, 0)])

    ahead, above, below, theirs = pl.pallas_call(
        halo_kernel,
        out_shape=[shape(len(PARTS[name][0]) * 8 + 8) for name in ("ahead", "above", "below")]
        + [shape(8, ())],
        in_specs=[vmem] * 2,
        out_specs=[vmem] * 4,
        compiler_params=params,
    )(own, theirs)
    ahead = lax.ppermute(ahead, AXES, shift_perm(0, 1))
    above = lax.ppermute(above, AXES, shift_perm(1, 0))
    below = lax.ppermute(below, AXES, shift_perm(-1, 0))

    partial = pl.pallas_call(
        kernel,
        out_shape=shape(256, ()),
        in_specs=[vmem] * 7,
        out_specs=vmem,
        compiler_params=params,
    )(column_order[None], jnp.repeat(column_order, 2)[None], theirs, own, ahead, above, below)
    terms = lax.all_to_all(partial, AXES, split_axis=0, concat_axis=0, tiled=True)
    return jnp.sum(terms, axis=0, keepdims=True)


def solution(mesh):
    in_specs = (
        P("trial", "slab", None, None),
        P("trial"),
        P("slab", None, None),
        P("trial", "slab", None, None),
        P("freq", None),
        P("freq"),
        P(),
    )
    out_specs = P(("trial", "slab"), None)
    return jax.shard_map(local, mesh=mesh, in_specs=in_specs, out_specs=out_specs, check_vma=False)
```

```python
import functools
import math

import jax
import jax.numpy as jnp
from jax import lax
from jax.experimental import pallas as pl
from jax.experimental.pallas import tpu as pltpu
from jax.sharding import PartitionSpec as P

AXES = ("trial", "slab", "freq")
HOP = 1.0 / 9.0

TILES = [(0, 0), (0, 1), (0, 2), (0, 3), (1, 0), (1, 1), (1, 2), (1, 3), "o", "e"]
ORB = TILES.index("o") * 8
EXTRA = TILES.index("e") * 8
OWN = [(row, plane) for row in range(2) for plane in range(4)]
PARTS = {
    "ahead": ([(row, plane) for row in range(2) for plane in range(3)], 0, 4),
    "above": ([(0, 0), (0, 1), (0, 2), (0, 3), (1, 0), (1, 1), (1, 3)], 2, 0),
    "below": ([(1, 0), (1, 1), (1, 2), (1, 3), (0, 2), (0, 3)], -2, 0),
}
AHEAD = PARTS["ahead"][0]


def pieces():
    table = {}
    for rp in OWN:
        table[rp] = ("own", TILES.index(rp) * 8, ORB + OWN.index(rp))
    for name, (taken, drow, dplane) in PARTS.items():
        for k, rp in enumerate(taken):
            orb = k if name == "ahead" else OWN.index(rp)
            table[(rp[0] + drow, rp[1] + dplane)] = (name, k * 8, len(taken) * 8 + orb)
    return table


def pairs():
    ahead = [(row, plane + 4) for row, plane in AHEAD]
    table = {}

    def near(a, b):
        return abs(a[0] - b[0]) + abs(a[1] - b[1]) <= 3

    def add(a, b):
        if near(a, b):
            table.setdefault(a, []).append(b)

    for n, a in enumerate(OWN):
        table.setdefault(a, []).append(a)
        for b in OWN[n + 1 :]:
            add(a, b)
        for b in ahead:
            add(a, b)
        for plane in range(4):
            add(a, (2, plane))
        if a[0] == 1:
            for plane in range(4):
                add(a, (-1, plane))
        if a in ((0, 0), (0, 1), (0, 3)):
            add(a, (3, a[1]))
        if a == (1, 2):
            add(a, (-2, 2))
    for a in ahead:
        if a[1] == 4:
            add(a, a)
        if a[0] == 0:
            others = [(-1, plane) for plane in range(4)] + [(2, 3), (-2, 3)]
        else:
            others = [(2, plane) for plane in range(4)] + [(-1, 3), (3, 3)]
        for b in others:
            add(a, b)
    for plane in range(4):
        add((-1, plane), (2, plane))
    return table


def half_of(slab, freq):
    return freq ^ (((slab + 1) // 2) & 1)


def pack_kernel(energy, cheb, shift, trials_hbm, orbital_hbm, potential_hbm, out_ref, scalars_ref, trials, orbital, potential, sems):
    trial, slab, freq = (lax.axis_index(a) for a in AXES)
    half = freq ^ (lax.div(slab + 1, 2) & 1)
    rows = pl.ds(pl.multiple_of(half * 32, 32), 32)
    copies = [
        pltpu.make_async_copy(source, target, sems.at[n])
        for n, (source, target) in enumerate(
            [
                (trials_hbm.at[:, rows, :], trials.reshape(32, 32, 128)),
                (orbital_hbm.at[:, rows, :], orbital.reshape(4, 32, 128)),
                (potential_hbm, potential.reshape(4, 64, 128)),
            ]
        )
    ]
    for copy in copies:
        copy.start()
    row_of = lax.broadcasted_iota(jnp.int32, (8, 128), 0)
    scalars = jnp.where(row_of == 0, energy[0], 0.0)
    for n, value in enumerate([cheb[0, 0], cheb[0, 1], cheb[0, 2], cheb[0, 3], shift[0]]):
        scalars = jnp.where(row_of == n + 2, value, scalars)
    scalars_ref[...] = scalars
    for copy in copies:
        copy.wait()
    for t in range(16):
        for k, tile in enumerate(TILES):
            if tile == "o":
                for row in range(2):
                    out_ref[t, k * 8 + 4 * row : k * 8 + 4 * row + 4, :] = orbital[pl.ds(2 * t + row, 4, stride=32), :]
            elif tile == "e":
                y = jnp.clip(half * 32 + 2 * t + lax.rem(trial, 4) - 1, 0, 63)
                at = potential[pl.ds(lax.div(trial, 4) * 64 + y, 1), :]
                out_ref[t, k * 8 : k * 8 + 8, :] = jnp.where(row_of == 1, at, scalars)
            else:
                out_ref[t, k * 8 : k * 8 + 8, :] = trials[pl.ds(tile[1] * 32 + 2 * t + tile[0], 8, stride=128), :]


def halo_kernel(own, theirs, ahead, above, below, theirs_ref):
    theirs_ref[...] = theirs[...]
    for name, ref in (("ahead", ahead), ("above", above), ("below", below)):
        taken = PARTS[name][0]
        for k, rp in enumerate(taken):
            start = TILES.index(rp) * 8
            ref[:, k * 8 : k * 8 + 8, :] = own[:, start : start + 8, :]
        if name != "ahead":
            ref[:, len(taken) * 8 :, :] = own[:, ORB : ORB + 8, :]
    last = [ORB + OWN.index(rp) for rp in AHEAD] + [EXTRA + 1, EXTRA + 1]
    for k, row in enumerate(last):
        ahead[:, 48 + k : 49 + k, :] = own[:, row : row + 1, :]


STAGES = (("own",), ("own", "ahead"), ("own", "ahead", "above", "below"))


def stage_of(where, a, b, dz):
    names = {where[a][0], where[b][0]}
    if a == b and dz == 0 and a[1] == 3:
        names.add("ahead")
    return next(n for n, held in enumerate(STAGES) if names <= set(held))


def halves(x):
    high = x.astype(jnp.bfloat16)
    return high, (x - high.astype(jnp.float32)).astype(jnp.bfloat16)


def thirds(x):
    high = x.astype(jnp.bfloat16)
    middle, low = halves(x - high.astype(jnp.float32))
    return high, middle, low


def product(lefts, rights, left_dim, right_dim):
    return lax.dot_general(
        jnp.concatenate(lefts, axis=left_dim), jnp.concatenate(rights, axis=right_dim),
        (((left_dim,), (right_dim,)), ((), ())), preferred_element_type=jnp.float32,
    )


def kernel(stage, *args):
    count = 2 if stage == 0 else 1
    out_ref, *pick_ref = args[-count:]
    args = args[:-count]
    refs = dict(zip(STAGES[stage], args[-len(STAGES[stage]) :]))
    own, ahead, theirs = refs["own"], refs.get("ahead"), args[0]
    where = pieces()
    lane = lax.broadcasted_iota(jnp.int32, (8, 128), 1)
    trial_index, slab, freq = (lax.axis_index(a) for a in AXES)
    block = (freq ^ (lax.div(slab + 1, 2) & 1)) * 16 + trial_index

    energy = own[:, EXTRA, :]
    a0 = a1 = a2 = a3 = jnp.zeros((16, 128), jnp.float32)
    for ref, first in ((own.at[0], EXTRA + 2), (theirs, 2)):
        k0, k1, k2, k3, shift = [ref[first + n : first + n + 1, :] for n in range(5)]
        c = (energy + shift) / 4.5
        b0, b1, b2, b3 = k0 - k2, k1 - 3.0 * k3, 2.0 * k2, 4.0 * k3
        a3 = a3 + b3
        a2 = a2 + (b2 - 3.0 * c * b3)
        a1 = a1 + (b1 - 2.0 * c * b2 + 3.0 * c * c * b3)
        a0 = a0 + (b0 - c * b1 + c * c * b2 - c * c * c * b3)
    amp = [a0, a1, a2, a3]

    orb = {}

    def orbital(rp):
        if rp not in orb:
            name, _, row = where[rp]
            orb[rp] = refs[name][:, row, :]
        return orb[rp]

    def trial(rp):
        name, row, _ = where[rp]
        return refs[name][:, row : row + 8, :]

    def turn(x, dz):
        return x if dz == 0 else pltpu.roll(x, dz % 128, x.ndim - 1)

    def inside_row(row):
        y = block * 2 + row
        return ((y >= 0) & (y < 64)).astype(jnp.float32)

    def inside_plane(plane):
        x = slab * 4 + plane
        return ((x >= 0) & (x < 32)).astype(jnp.float32)

    def inside_z(dz):
        return ((lane + dz >= 0) & (lane + dz < 128)).astype(jnp.float32)

    pot = {}

    def potential(row, plane):
        if (row, plane) not in pot:
            ref, at = (own, EXTRA + 1) if plane < 4 else (ahead, 54)
            source = plane % 4 * 4 + row + 1
            pot[(row, plane)] = jnp.broadcast_to(ref[source, at : at + 1, :] / 4.5, (8, 128))
        return pot[(row, plane)]

    ones = jnp.ones((8, 128), jnp.float32)

    def powers(a, b, dz):
        dy, dx = b[0] - a[0], b[1] - a[1]
        step = (dx, dy, dz)
        dist = abs(dx) + abs(dy) + abs(dz)
        ways = math.factorial(dist)
        for s in step:
            ways //= math.factorial(abs(s))
        if dist == 3:
            return None, None, None, -(HOP**3) * ways
        vq = potential(*b) if dist < 3 else None
        vp = turn(potential(*a), dz)
        if dist == 2:
            total = float(ways) * (vp + vq)
            moves = [n for n in range(3) if step[n] != 0]
            for n in moves:
                part = [0, 0, 0]
                part[n] = 1 if step[n] > 0 else -1
                mid = potential(a[0] + part[1], a[1] + part[0])
                total = total + turn(mid, dz - part[2])
            return None, None, HOP**2 * ways, HOP**2 * total
        if dist == 1:
            if dz != 0:
                across = inside_row(a[0] - 1) + inside_row(a[0] + 1) + inside_plane(a[1] - 1) + inside_plane(a[1] + 1)
                along = inside_z(-2 * dz) + inside_z(dz)
            else:
                across = inside_z(1) + inside_z(-1)
                if dy != 0:
                    across = across + inside_plane(a[1] - 1) + inside_plane(a[1] + 1)
                    along = inside_row(a[0] - dy) + inside_row(b[0] + dy)
                else:
                    across = across + inside_row(a[0] - 1) + inside_row(a[0] + 1)
                    along = inside_plane(a[1] - dx) + inside_plane(b[1] + dx)
            walks = (3.0 * across + along + 1.0) * ones
            return None, -HOP, -HOP * (vp + vq), -HOP * (vp * vp + vp * vq + vq * vq) - HOP**3 * walks
        if a[1] == 4:
            return None, None, None, HOP**2 * potential(a[0], 3)
        around = [(a[0] - 1, a[1]), (a[0] + 1, a[1]), (a[0], a[1] - 1), (a[0], a[1] + 1)]
        degree = inside_z(1) + inside_z(-1)
        near = inside_z(-1) * turn(vp, 1) + inside_z(1) * turn(vp, -1)
        for row, plane in around:
            here = inside_row(row) * inside_plane(plane)
            degree = degree + here
            if plane >= 0:
                near = near + here * potential(row, plane)
        square = vp * vp
        return 1.0, vp, square + HOP**2 * degree, vp * square + HOP**2 * (2.0 * degree * vp + near)

    def coefficient(a, b, dz, left):
        right = orbital(b)
        total = None
        for m, h in enumerate(powers(a, b, dz)):
            if h is None:
                continue
            both = left[m] * right
            term = (both[:8] + both[8:]) * h
            total = term if total is None else total + term
        for s in (4, 2, 1):
            total = total + pltpu.roll(total, s, 0)
        if a == b and dz == 0:
            total = total * 0.5
        if dz != 0:
            total = total * inside_z(-dz)
        return total

    if stage == 0:
        gram = jnp.zeros((128, 128), jnp.float32)
        rows = lax.broadcasted_iota(jnp.int32, (128, 128), 0)
        pick_ref[0][...] = (args[1][...] == rows).astype(jnp.float32)
    else:
        gram = args[1][...]
    lefts, sides = [], []
    for a, rights in pairs().items():
        response = None
        for dz in range(-3, 4):
            todo = []
            for b in rights:
                dist = abs(a[0] - b[0]) + abs(a[1] - b[1]) + abs(dz)
                if dist > 3 or stage_of(where, a, b, dz) != stage:
                    continue
                if a != b or dz == 0 or (dz > 0 and a[1] < 4):
                    todo.append((b, dist))
            if not todo:
                continue
            moved = turn(orbital(a), dz)
            least = min(dist for _, dist in todo)
            left = [moved * amp[m] if m >= least else None for m in range(4)]
            acc = None
            for b, _ in todo:
                term = coefficient(a, b, dz, left)[None] * trial(b)
                acc = term if acc is None else acc + term
            acc = turn(acc.reshape(128, 128), -dz)
            response = acc if response is None else response + acc
        if response is None:
            continue
        high, low = halves(trial(a).reshape(128, 128))
        other, rest = halves(response)
        lefts += [high, high, low]
        sides += [other, rest, other]
        if len(lefts) == 6:
            gram = gram + product(lefts, sides, 1, 1)
            lefts, sides = [], []
    if lefts:
        gram = gram + product(lefts, sides, 1, 1)

    if stage < 2:
        out_ref[...] = gram
        return
    gram = (gram + gram.T) * (1.0 / math.sqrt(32 * 64 * 128 * 16))
    pick = args[2][...].astype(jnp.bfloat16)
    gram = product(thirds(gram), [pick] * 3, 1, 0)
    gram = product([pick] * 3, thirds(gram), 0, 0)
    for n in range(2):
        out_ref[pl.ds(n, 128, stride=2), :] = gram


def device(block, slab):
    return ((block % 16) * 8 + slab) * 2 + half_of(slab, block // 16)


def shift_perm(step, dslab):
    return [
        (device(block + step, slab + dslab), device(block, slab))
        for block in range(32)
        for slab in range(8)
        if 0 <= block + step < 32 and slab + dslab < 8
    ]


def local(orbitals, energies, potential, trials, cheb, shifts, column_order):
    smem = pl.BlockSpec(memory_space=pltpu.SMEM)
    vmem = pl.BlockSpec(memory_space=pltpu.VMEM)
    params = pltpu.CompilerParams(vmem_limit_bytes=32 * 1024 * 1024)

    def shape(rows, lead=(16,)):
        return jax.ShapeDtypeStruct((*lead, rows, 128), jnp.float32)

    send, scalars = pl.pallas_call(
        pack_kernel,
        out_shape=[shape(len(TILES) * 8), shape(8, ())],
        in_specs=[smem] * 3 + [pl.BlockSpec(memory_space=pltpu.HBM)] * 3,
        out_specs=[vmem] * 2,
        scratch_shapes=[
            pltpu.VMEM((1024, 128), jnp.float32),
            pltpu.VMEM((128, 128), jnp.float32),
            pltpu.VMEM((256, 128), jnp.float32),
            pltpu.SemaphoreType.DMA((3,)),
        ],
        compiler_params=pltpu.CompilerParams(vmem_limit_bytes=60 * 1024 * 1024),
    )(energies, cheb, shifts, trials.reshape(32, 64, 128), orbitals[0], potential)
    own = lax.all_to_all(send, "trial", split_axis=0, concat_axis=0, tiled=True)

    theirs = lax.ppermute(scalars, "freq", [(0, 1), (1, 0)])

    ahead, above, below, theirs = pl.pallas_call(
        halo_kernel,
        out_shape=[shape(len(PARTS[name][0]) * 8 + 8) for name in ("ahead", "above", "below")]
        + [shape(8, ())],
        in_specs=[vmem] * 2,
        out_specs=[vmem] * 4,
        compiler_params=params,
    )(own, theirs)
    ahead = lax.ppermute(ahead, AXES, shift_perm(0, 1))
    above = lax.ppermute(above, AXES, shift_perm(1, 0))
    below = lax.ppermute(below, AXES, shift_perm(-1, 0))

    arrays = {"own": own, "ahead": ahead, "above": above, "below": below}
    partial = pick = None
    for stage, names in enumerate(STAGES):
        operands = [theirs, column_order[None] if stage == 0 else partial]
        if stage == 2:
            operands.append(pick)
        operands += [arrays[name] for name in names]
        shapes = [shape(256 if stage == 2 else 128, ())]
        if stage == 0:
            shapes.append(shape(128, ()))
        partial, *rest = pl.pallas_call(
            functools.partial(kernel, stage),
            out_shape=shapes,
            in_specs=[vmem] * len(operands),
            out_specs=[vmem] * len(shapes),
            compiler_params=params,
            cost_estimate=pl.CostEstimate(flops=2 * 10**9, bytes_accessed=3 * 2**20, transcendentals=0),
        )(*operands)
        pick = rest[0] if rest else pick
    terms = lax.all_to_all(partial, AXES, split_axis=0, concat_axis=0, tiled=True)
    return jnp.sum(terms, axis=0, keepdims=True)


def solution(mesh):
    in_specs = (
        P("trial", "slab", None, None),
        P("trial"),
        P("slab", None, None),
        P("trial", "slab", None, None),
        P("freq", None),
        P("freq"),
        P(),
    )
    out_specs = P(("trial", "slab"), None)
    return jax.shard_map(local, mesh=mesh, in_specs=in_specs, out_specs=out_specs, check_vma=False)
```

```python
import functools
import math

import jax
import jax.numpy as jnp
from jax import lax
from jax.experimental import pallas as pl
from jax.experimental.pallas import tpu as pltpu
from jax.sharding import PartitionSpec as P

AXES = ("trial", "slab", "freq")
HOP = 1.0 / 9.0

TILES = [(0, 0), (0, 1), (0, 2), (0, 3), (1, 0), (1, 1), (1, 2), (1, 3), "o", "e"]
ORB = TILES.index("o") * 8
EXTRA = TILES.index("e") * 8
SENT = EXTRA + 2
OWN = [(row, plane) for row in range(2) for plane in range(4)]
PARTS = {
    "ahead": ([(row, plane) for row in range(2) for plane in range(3)], 0, 4),
    "above": ([(0, 0), (0, 1), (0, 2), (0, 3), (1, 0), (1, 1), (1, 3)], 2, 0),
    "below": ([(1, 0), (1, 1), (1, 2), (1, 3), (0, 2), (0, 3)], -2, 0),
}
AHEAD = PARTS["ahead"][0]


def pieces():
    table = {}
    for rp in OWN:
        table[rp] = ("own", TILES.index(rp) * 8, ORB + OWN.index(rp))
    for name, (taken, drow, dplane) in PARTS.items():
        for k, rp in enumerate(taken):
            orb = k if name == "ahead" else OWN.index(rp)
            table[(rp[0] + drow, rp[1] + dplane)] = (name, k * 8, len(taken) * 8 + orb)
    return table


def pairs():
    ahead = [(row, plane + 4) for row, plane in AHEAD]
    table = {}

    def near(a, b):
        return abs(a[0] - b[0]) + abs(a[1] - b[1]) <= 3

    def add(a, b):
        if near(a, b):
            table.setdefault(a, []).append(b)

    for n, a in enumerate(OWN):
        table.setdefault(a, []).append(a)
        for b in OWN[n + 1 :]:
            add(a, b)
        for b in ahead:
            add(a, b)
        for plane in range(4):
            add(a, (2, plane))
        if a[0] == 1:
            for plane in range(4):
                add(a, (-1, plane))
        if a in ((0, 0), (0, 1), (0, 3)):
            add(a, (3, a[1]))
        if a == (1, 2):
            add(a, (-2, 2))
    for a in ahead:
        if a[1] == 4:
            add(a, a)
        if a[0] == 0:
            others = [(-1, plane) for plane in range(4)] + [(2, 3), (-2, 3)]
        else:
            others = [(2, plane) for plane in range(4)] + [(-1, 3), (3, 3)]
        for b in others:
            add(a, b)
    for plane in range(4):
        add((-1, plane), (2, plane))
    return table


def half_of(slab, freq):
    return freq ^ (((slab + 1) // 2) & 1)


def pack_kernel(energy, cheb, shift, trials_hbm, orbital_hbm, potential_hbm, out_ref, scalars_ref, trials, orbital, potential, sems):
    trial, slab, freq = (lax.axis_index(a) for a in AXES)
    half = freq ^ (lax.div(slab + 1, 2) & 1)
    rows = pl.ds(pl.multiple_of(half * 32, 32), 32)
    copies = [
        pltpu.make_async_copy(source, target, sems.at[n])
        for n, (source, target) in enumerate(
            [
                (trials_hbm.at[:, rows, :], trials.reshape(32, 32, 128)),
                (orbital_hbm.at[:, rows, :], orbital.reshape(4, 32, 128)),
                (potential_hbm, potential.reshape(4, 64, 128)),
            ]
        )
    ]
    for copy in copies:
        copy.start()
    row_of = lax.broadcasted_iota(jnp.int32, (8, 128), 0)
    scalars = jnp.where(row_of == 0, energy[0], 0.0)
    for n, value in enumerate([cheb[0, 0], cheb[0, 1], cheb[0, 2], cheb[0, 3], shift[0]]):
        scalars = jnp.where(row_of == n + 2, value, scalars)
    scalars_ref[...] = scalars
    for copy in copies:
        copy.wait()
    for t in range(16):
        base = t * SENT
        for k, tile in enumerate(TILES):
            if tile == "o":
                for row in range(2):
                    out_ref[base + k * 8 + 4 * row : base + k * 8 + 4 * row + 4, :] = orbital[
                        pl.ds(2 * t + row, 4, stride=32), :
                    ]
            elif tile == "e":
                y = jnp.clip(half * 32 + 2 * t + lax.rem(trial, 4) - 1, 0, 63)
                at = potential[pl.ds(lax.div(trial, 4) * 64 + y, 1), :]
                out_ref[base + k * 8 : base + k * 8 + 2, :] = jnp.where(row_of == 1, at, scalars)[:2]
            else:
                out_ref[base + k * 8 : base + k * 8 + 8, :] = trials[
                    pl.ds(tile[1] * 32 + 2 * t + tile[0], 8, stride=128), :
                ]


def halo_kernel(raw, ours, theirs, ahead, above, below, theirs_ref, own):
    theirs_ref[...] = theirs[...]
    for s in range(16):
        for first in range(0, SENT, 8):
            size = min(8, SENT - first)
            own[s, first : first + size, :] = raw[s * SENT + first : s * SENT + first + size, :]
        own[s, SENT:, :] = ours[2:, :]
    for name, ref in (("ahead", ahead), ("above", above), ("below", below)):
        taken = PARTS[name][0]
        for k, rp in enumerate(taken):
            start = TILES.index(rp) * 8
            ref[:, k * 8 : k * 8 + 8, :] = own[:, start : start + 8, :]
        if name != "ahead":
            ref[:, len(taken) * 8 :, :] = own[:, ORB : ORB + 8, :]
    last = [ORB + OWN.index(rp) for rp in AHEAD] + [EXTRA + 1, EXTRA + 1]
    for k, row in enumerate(last):
        ahead[:, 48 + k : 49 + k, :] = own[:, row : row + 1, :]


STAGES = (("own",), ("own", "ahead"), ("own", "ahead", "above", "below"))


def stage_of(where, a, b, dz):
    names = {where[a][0], where[b][0]}
    if a == b and dz == 0 and a[1] == 3:
        names.add("ahead")
    return next(n for n, held in enumerate(STAGES) if names <= set(held))


def halves(x):
    high = x.astype(jnp.bfloat16)
    return high, (x - high.astype(jnp.float32)).astype(jnp.bfloat16)


def thirds(x):
    high = x.astype(jnp.bfloat16)
    middle, low = halves(x - high.astype(jnp.float32))
    return high, middle, low


def product(lefts, rights, left_dim, right_dim):
    return lax.dot_general(
        jnp.concatenate(lefts, axis=left_dim), jnp.concatenate(rights, axis=right_dim),
        (((left_dim,), (right_dim,)), ((), ())), preferred_element_type=jnp.float32,
    )


def kernel(stage, *args):
    count = 2 if stage == 0 else 1
    out_ref, *pick_ref = args[-count:]
    args = args[:-count]
    refs = dict(zip(STAGES[stage], args[-len(STAGES[stage]) :]))
    own, ahead, theirs = refs["own"], refs.get("ahead"), args[0]
    where = pieces()
    lane = lax.broadcasted_iota(jnp.int32, (8, 128), 1)
    trial_index, slab, freq = (lax.axis_index(a) for a in AXES)
    block = (freq ^ (lax.div(slab + 1, 2) & 1)) * 16 + trial_index

    energy = own[:, EXTRA, :]
    a0 = a1 = a2 = a3 = jnp.zeros((16, 128), jnp.float32)
    for ref, first in ((own.at[0], EXTRA + 2), (theirs, 2)):
        k0, k1, k2, k3, shift = [ref[first + n : first + n + 1, :] for n in range(5)]
        c = (energy + shift) / 4.5
        b0, b1, b2, b3 = k0 - k2, k1 - 3.0 * k3, 2.0 * k2, 4.0 * k3
        a3 = a3 + b3
        a2 = a2 + (b2 - 3.0 * c * b3)
        a1 = a1 + (b1 - 2.0 * c * b2 + 3.0 * c * c * b3)
        a0 = a0 + (b0 - c * b1 + c * c * b2 - c * c * c * b3)
    amp = [a0, a1, a2, a3]

    orb = {}

    def orbital(rp):
        if rp not in orb:
            name, _, row = where[rp]
            orb[rp] = refs[name][:, row, :]
        return orb[rp]

    def trial(rp):
        name, row, _ = where[rp]
        return refs[name][:, row : row + 8, :]

    def turn(x, dz):
        return x if dz == 0 else pltpu.roll(x, dz % 128, x.ndim - 1)

    def inside_row(row):
        y = block * 2 + row
        return ((y >= 0) & (y < 64)).astype(jnp.float32)

    def inside_plane(plane):
        x = slab * 4 + plane
        return ((x >= 0) & (x < 32)).astype(jnp.float32)

    def inside_z(dz):
        return ((lane + dz >= 0) & (lane + dz < 128)).astype(jnp.float32)

    pot = {}

    def potential(row, plane):
        if (row, plane) not in pot:
            ref, at = (own, EXTRA + 1) if plane < 4 else (ahead, 54)
            source = plane % 4 * 4 + row + 1
            pot[(row, plane)] = jnp.broadcast_to(ref[source, at : at + 1, :] / 4.5, (8, 128))
        return pot[(row, plane)]

    ones = jnp.ones((8, 128), jnp.float32)

    def powers(a, b, dz):
        dy, dx = b[0] - a[0], b[1] - a[1]
        step = (dx, dy, dz)
        dist = abs(dx) + abs(dy) + abs(dz)
        ways = math.factorial(dist)
        for s in step:
            ways //= math.factorial(abs(s))
        if dist == 3:
            return None, None, None, -(HOP**3) * ways
        vq = potential(*b) if dist < 3 else None
        vp = turn(potential(*a), dz)
        if dist == 2:
            total = float(ways) * (vp + vq)
            moves = [n for n in range(3) if step[n] != 0]
            for n in moves:
                part = [0, 0, 0]
                part[n] = 1 if step[n] > 0 else -1
                mid = potential(a[0] + part[1], a[1] + part[0])
                total = total + turn(mid, dz - part[2])
            return None, None, HOP**2 * ways, HOP**2 * total
        if dist == 1:
            if dz != 0:
                across = inside_row(a[0] - 1) + inside_row(a[0] + 1) + inside_plane(a[1] - 1) + inside_plane(a[1] + 1)
                along = inside_z(-2 * dz) + inside_z(dz)
            else:
                across = inside_z(1) + inside_z(-1)
                if dy != 0:
                    across = across + inside_plane(a[1] - 1) + inside_plane(a[1] + 1)
                    along = inside_row(a[0] - dy) + inside_row(b[0] + dy)
                else:
                    across = across + inside_row(a[0] - 1) + inside_row(a[0] + 1)
                    along = inside_plane(a[1] - dx) + inside_plane(b[1] + dx)
            walks = (3.0 * across + along + 1.0) * ones
            return None, -HOP, -HOP * (vp + vq), -HOP * (vp * vp + vp * vq + vq * vq) - HOP**3 * walks
        if a[1] == 4:
            return None, None, None, HOP**2 * potential(a[0], 3)
        around = [(a[0] - 1, a[1]), (a[0] + 1, a[1]), (a[0], a[1] - 1), (a[0], a[1] + 1)]
        degree = inside_z(1) + inside_z(-1)
        near = inside_z(-1) * turn(vp, 1) + inside_z(1) * turn(vp, -1)
        for row, plane in around:
            here = inside_row(row) * inside_plane(plane)
            degree = degree + here
            if plane >= 0:
                near = near + here * potential(row, plane)
        square = vp * vp
        return 1.0, vp, square + HOP**2 * degree, vp * square + HOP**2 * (2.0 * degree * vp + near)

    def coefficient(a, b, dz, left):
        right = orbital(b)
        total = None
        for m, h in enumerate(powers(a, b, dz)):
            if h is None:
                continue
            both = left[m] * right
            term = (both[:8] + both[8:]) * h
            total = term if total is None else total + term
        for s in (4, 2, 1):
            total = total + pltpu.roll(total, s, 0)
        if a == b and dz == 0:
            total = total * 0.5
        if dz != 0:
            total = total * inside_z(-dz)
        return total

    if stage == 0:
        gram = jnp.zeros((128, 128), jnp.float32)
        rows = lax.broadcasted_iota(jnp.int32, (128, 128), 0)
        pick_ref[0][...] = (args[1][...] == rows).astype(jnp.float32)
    else:
        gram = args[1][...]
    lefts, sides = [], []
    for a, rights in pairs().items():
        response = None
        for dz in range(-3, 4):
            todo = []
            for b in rights:
                dist = abs(a[0] - b[0]) + abs(a[1] - b[1]) + abs(dz)
                if dist > 3 or stage_of(where, a, b, dz) != stage:
                    continue
                if a != b or dz == 0 or (dz > 0 and a[1] < 4):
                    todo.append((b, dist))
            if not todo:
                continue
            moved = turn(orbital(a), dz)
            least = min(dist for _, dist in todo)
            left = [moved * amp[m] if m >= least else None for m in range(4)]
            acc = None
            for b, _ in todo:
                term = coefficient(a, b, dz, left)[None] * trial(b)
                acc = term if acc is None else acc + term
            acc = turn(acc.reshape(128, 128), -dz)
            response = acc if response is None else response + acc
        if response is None:
            continue
        high, low = halves(trial(a).reshape(128, 128))
        other, rest = halves(response)
        lefts += [high, high, low]
        sides += [other, rest, other]
        if len(lefts) == 6:
            gram = gram + product(lefts, sides, 1, 1)
            lefts, sides = [], []
    if lefts:
        gram = gram + product(lefts, sides, 1, 1)

    if stage < 2:
        out_ref[...] = gram
        return
    gram = (gram + gram.T) * (1.0 / math.sqrt(32 * 64 * 128 * 16))
    pick = args[2][...].astype(jnp.bfloat16)
    gram = product(thirds(gram), [pick] * 3, 1, 0)
    gram = product([pick] * 3, thirds(gram), 0, 0)
    for n in range(2):
        out_ref[pl.ds(n, 128, stride=2), :] = gram


def device(block, slab):
    return ((block % 16) * 8 + slab) * 2 + half_of(slab, block // 16)


def shift_perm(step, dslab):
    return [
        (device(block + step, slab + dslab), device(block, slab))
        for block in range(32)
        for slab in range(8)
        if 0 <= block + step < 32 and slab + dslab < 8
    ]


def local(orbitals, energies, potential, trials, cheb, shifts, column_order):
    smem = pl.BlockSpec(memory_space=pltpu.SMEM)
    vmem = pl.BlockSpec(memory_space=pltpu.VMEM)
    params = pltpu.CompilerParams(vmem_limit_bytes=32 * 1024 * 1024)

    def shape(rows, lead=(16,)):
        return jax.ShapeDtypeStruct((*lead, rows, 128), jnp.float32)

    send, scalars = pl.pallas_call(
        pack_kernel,
        out_shape=[shape(16 * SENT, ()), shape(8, ())],
        in_specs=[smem] * 3 + [pl.BlockSpec(memory_space=pltpu.HBM)] * 3,
        out_specs=[vmem] * 2,
        scratch_shapes=[
            pltpu.VMEM((1024, 128), jnp.float32),
            pltpu.VMEM((128, 128), jnp.float32),
            pltpu.VMEM((256, 128), jnp.float32),
            pltpu.SemaphoreType.DMA((3,)),
        ],
        compiler_params=pltpu.CompilerParams(vmem_limit_bytes=60 * 1024 * 1024),
    )(energies, cheb, shifts, trials.reshape(32, 64, 128), orbitals[0], potential)
    raw = lax.all_to_all(send.reshape(16 * SENT, 1, 128), "trial", split_axis=0, concat_axis=0, tiled=True)

    theirs = lax.ppermute(scalars, "freq", [(0, 1), (1, 0)])

    ahead, above, below, theirs, own = pl.pallas_call(
        halo_kernel,
        out_shape=[shape(len(PARTS[name][0]) * 8 + 8) for name in ("ahead", "above", "below")]
        + [shape(8, ()), shape(len(TILES) * 8)],
        in_specs=[vmem] * 3,
        out_specs=[vmem] * 5,
        compiler_params=params,
    )(raw.reshape(16 * SENT, 128), scalars, theirs)
    ahead = lax.ppermute(ahead, AXES, shift_perm(0, 1))
    above = lax.ppermute(above, AXES, shift_perm(1, 0))
    below = lax.ppermute(below, AXES, shift_perm(-1, 0))

    arrays = {"own": own, "ahead": ahead, "above": above, "below": below}
    partial = pick = None
    for stage, names in enumerate(STAGES):
        operands = [theirs, column_order[None] if stage == 0 else partial]
        if stage == 2:
            operands.append(pick)
        operands += [arrays[name] for name in names]
        shapes = [shape(256 if stage == 2 else 128, ())]
        if stage == 0:
            shapes.append(shape(128, ()))
        partial, *rest = pl.pallas_call(
            functools.partial(kernel, stage),
            out_shape=shapes,
            in_specs=[vmem] * len(operands),
            out_specs=[vmem] * len(shapes),
            compiler_params=params,
            cost_estimate=pl.CostEstimate(flops=2 * 10**9, bytes_accessed=3 * 2**20, transcendentals=0),
        )(*operands)
        pick = rest[0] if rest else pick
    terms = lax.all_to_all(partial, AXES, split_axis=0, concat_axis=0, tiled=True)
    return jnp.sum(terms, axis=0, keepdims=True)


def solution(mesh):
    in_specs = (
        P("trial", "slab", None, None),
        P("trial"),
        P("slab", None, None),
        P("trial", "slab", None, None),
        P("freq", None),
        P("freq"),
        P(),
    )
    out_specs = P(("trial", "slab"), None)
    return jax.shard_map(local, mesh=mesh, in_specs=in_specs, out_specs=out_specs, check_vma=False)
```

```python
import functools
import math

import jax
import jax.numpy as jnp
from jax import lax
from jax.experimental import pallas as pl
from jax.experimental.pallas import tpu as pltpu
from jax.sharding import PartitionSpec as P

AXES = ("trial", "slab", "freq")
HOP = 1.0 / 9.0

TILES = [(0, 0), (0, 1), (0, 2), (0, 3), (1, 0), (1, 1), (1, 2), (1, 3), "o", "e"]
ORB = TILES.index("o") * 8
EXTRA = TILES.index("e") * 8
SENT = EXTRA + 2
OWN = [(row, plane) for row in range(2) for plane in range(4)]
PARTS = {
    "ahead": ([(row, plane) for row in range(2) for plane in range(3)], 0, 4),
    "above": ([(0, 0), (0, 1), (0, 2), (0, 3), (1, 0), (1, 1), (1, 3)], 2, 0),
    "below": ([(1, 0), (1, 1), (1, 2), (1, 3), (0, 2), (0, 3)], -2, 0),
}
AHEAD = PARTS["ahead"][0]


def pieces():
    table = {}
    for rp in OWN:
        table[rp] = ("own", TILES.index(rp) * 8, ORB, OWN.index(rp))
    for name, (taken, drow, dplane) in PARTS.items():
        for k, rp in enumerate(taken):
            orb = k if name == "ahead" else OWN.index(rp)
            table[(rp[0] + drow, rp[1] + dplane)] = (name, k * 8, len(taken) * 8, orb)
    return table


def pairs():
    ahead = [(row, plane + 4) for row, plane in AHEAD]
    table = {}

    def near(a, b):
        return abs(a[0] - b[0]) + abs(a[1] - b[1]) <= 3

    def add(a, b):
        if near(a, b):
            table.setdefault(a, []).append(b)

    for n, a in enumerate(OWN):
        table.setdefault(a, []).append(a)
        for b in OWN[n + 1 :]:
            add(a, b)
        for b in ahead:
            add(a, b)
        for plane in range(4):
            add(a, (2, plane))
        if a[0] == 1:
            for plane in range(4):
                add(a, (-1, plane))
        if a in ((0, 0), (0, 1), (0, 3)):
            add(a, (3, a[1]))
        if a == (1, 2):
            add(a, (-2, 2))
    for a in ahead:
        if a[1] == 4:
            add(a, a)
        if a[0] == 0:
            others = [(-1, plane) for plane in range(4)] + [(2, 3), (-2, 3)]
        else:
            others = [(2, plane) for plane in range(4)] + [(-1, 3), (3, 3)]
        for b in others:
            add(a, b)
    for plane in range(4):
        add((-1, plane), (2, plane))
    return table


def half_of(slab, freq):
    return freq ^ (((slab + 1) // 2) & 1)


def pack_kernel(energy, cheb, shift, trials_hbm, orbital_hbm, potential_hbm, out_ref, scalars_ref, trials, orbital, potential, sems):
    trial, slab, freq = (lax.axis_index(a) for a in AXES)
    half = freq ^ (lax.div(slab + 1, 2) & 1)
    rows = pl.ds(pl.multiple_of(half * 32, 32), 32)
    copies = [
        pltpu.make_async_copy(source, target, sems.at[n])
        for n, (source, target) in enumerate(
            [
                (trials_hbm.at[:, rows, :], trials.reshape(32, 32, 128)),
                (orbital_hbm.at[:, rows, :], orbital.reshape(4, 32, 128)),
                (potential_hbm, potential.reshape(4, 64, 128)),
            ]
        )
    ]
    for copy in copies:
        copy.start()
    row_of = lax.broadcasted_iota(jnp.int32, (8, 128), 0)
    scalars = jnp.where(row_of == 0, energy[0], 0.0)
    for n, value in enumerate([cheb[0, 0], cheb[0, 1], cheb[0, 2], cheb[0, 3], shift[0]]):
        scalars = jnp.where(row_of == n + 2, value, scalars)
    scalars_ref[...] = scalars
    for copy in copies:
        copy.wait()
    for t in range(16):
        base = t * SENT
        for k, tile in enumerate(TILES):
            if tile == "o":
                for row in range(2):
                    out_ref[base + k * 8 + 4 * row : base + k * 8 + 4 * row + 4, :] = orbital[
                        pl.ds(2 * t + row, 4, stride=32), :
                    ]
            elif tile == "e":
                y = jnp.clip(half * 32 + 2 * t + lax.rem(trial, 4) - 1, 0, 63)
                at = potential[pl.ds(lax.div(trial, 4) * 64 + y, 1), :]
                out_ref[base + k * 8 : base + k * 8 + 2, :] = jnp.where(row_of == 1, at, scalars)[:2]
            else:
                out_ref[base + k * 8 : base + k * 8 + 8, :] = trials[
                    pl.ds(tile[1] * 32 + 2 * t + tile[0], 8, stride=128), :
                ]


def halo_kernel(raw, ours, theirs, ahead, above, below, theirs_ref, own):
    theirs_ref[...] = theirs[...]
    for s in range(16):
        for first in range(0, SENT, 8):
            size = min(8, SENT - first)
            own[s, first : first + size, :] = raw[s * SENT + first : s * SENT + first + size, :]
        own[s, SENT:, :] = ours[2:, :]
    for k in range(8):
        orbs = raw[pl.ds(ORB + k, 16, stride=SENT), :]
        own[2 * k, ORB : ORB + 8, :] = orbs[:8]
        own[2 * k + 1, ORB : ORB + 8, :] = orbs[8:]
    for name, ref in (("ahead", ahead), ("above", above), ("below", below)):
        taken = PARTS[name][0]
        for k, rp in enumerate(taken):
            start = TILES.index(rp) * 8
            ref[:, k * 8 : k * 8 + 8, :] = own[:, start : start + 8, :]
        if name != "ahead":
            ref[:, len(taken) * 8 :, :] = own[:, ORB : ORB + 8, :]
    for k, rp in enumerate(AHEAD):
        start = 2 * OWN.index(rp)
        ahead[2 * k : 2 * k + 2, 48:, :] = own[start : start + 2, ORB : ORB + 8, :]
    levels = raw[pl.ds(EXTRA + 1, 16, stride=SENT), :]
    for k in (12, 14):
        ahead[k, 48:, :] = levels[:8]
        ahead[k + 1, 48:, :] = levels[8:]


STAGES = (("own",), ("own", "ahead"), ("own", "ahead", "above", "below"))


def stage_of(where, a, b, dz):
    names = {where[a][0], where[b][0]}
    if a == b and dz == 0 and a[1] == 3:
        names.add("ahead")
    return next(n for n, held in enumerate(STAGES) if names <= set(held))


def halves(x):
    high = x.astype(jnp.bfloat16)
    return high, (x - high.astype(jnp.float32)).astype(jnp.bfloat16)


def thirds(x):
    high = x.astype(jnp.bfloat16)
    middle, low = halves(x - high.astype(jnp.float32))
    return high, middle, low


def product(lefts, rights, left_dim, right_dim):
    return lax.dot_general(
        jnp.concatenate(lefts, axis=left_dim), jnp.concatenate(rights, axis=right_dim),
        (((left_dim,), (right_dim,)), ((), ())), preferred_element_type=jnp.float32,
    )


def kernel(stage, *args):
    count = 2 if stage == 0 else 1
    out_ref, *pick_ref = args[-count:]
    args = args[:-count]
    refs = dict(zip(STAGES[stage], args[-len(STAGES[stage]) :]))
    own, ahead, theirs = refs["own"], refs.get("ahead"), args[0]
    where = pieces()
    lane = lax.broadcasted_iota(jnp.int32, (8, 128), 1)
    trial_index, slab, freq = (lax.axis_index(a) for a in AXES)
    block = (freq ^ (lax.div(slab + 1, 2) & 1)) * 16 + trial_index

    energy = own[:, EXTRA, :]
    a0 = a1 = a2 = a3 = jnp.zeros((16, 128), jnp.float32)
    for ref, first in ((own.at[0], EXTRA + 2), (theirs, 2)):
        k0, k1, k2, k3, shift = [ref[first + n : first + n + 1, :] for n in range(5)]
        c = (energy + shift) / 4.5
        b0, b1, b2, b3 = k0 - k2, k1 - 3.0 * k3, 2.0 * k2, 4.0 * k3
        a3 = a3 + b3
        a2 = a2 + (b2 - 3.0 * c * b3)
        a1 = a1 + (b1 - 2.0 * c * b2 + 3.0 * c * c * b3)
        a0 = a0 + (b0 - c * b1 + c * c * b2 - c * c * c * b3)
    amp = [a0, a1, a2, a3]

    orb = {}

    def orbital(rp):
        if rp not in orb:
            name, _, row, k = where[rp]
            orb[rp] = jnp.concatenate([refs[name][2 * k + n, row : row + 8, :] for n in range(2)], axis=0)
        return orb[rp]

    def trial(rp):
        name, row, _, _ = where[rp]
        return refs[name][:, row : row + 8, :]

    def turn(x, dz):
        return x if dz == 0 else pltpu.roll(x, dz % 128, x.ndim - 1)

    def inside_row(row):
        y = block * 2 + row
        return ((y >= 0) & (y < 64)).astype(jnp.float32)

    def inside_plane(plane):
        x = slab * 4 + plane
        return ((x >= 0) & (x < 32)).astype(jnp.float32)

    def inside_z(dz):
        return ((lane + dz >= 0) & (lane + dz < 128)).astype(jnp.float32)

    pot = {}

    def potential(row, plane):
        if (row, plane) not in pot:
            source = plane % 4 * 4 + row + 1
            if plane < 4:
                at = own[source, EXTRA + 1 : EXTRA + 2, :]
            else:
                at = ahead[12 + source // 8, 48 + source % 8 : 49 + source % 8, :]
            pot[(row, plane)] = jnp.broadcast_to(at / 4.5, (8, 128))
        return pot[(row, plane)]

    ones = jnp.ones((8, 128), jnp.float32)

    def powers(a, b, dz):
        dy, dx = b[0] - a[0], b[1] - a[1]
        step = (dx, dy, dz)
        dist = abs(dx) + abs(dy) + abs(dz)
        ways = math.factorial(dist)
        for s in step:
            ways //= math.factorial(abs(s))
        if dist == 3:
            return None, None, None, -(HOP**3) * ways
        vq = potential(*b) if dist < 3 else None
        vp = turn(potential(*a), dz)
        if dist == 2:
            total = float(ways) * (vp + vq)
            moves = [n for n in range(3) if step[n] != 0]
            for n in moves:
                part = [0, 0, 0]
                part[n] = 1 if step[n] > 0 else -1
                mid = potential(a[0] + part[1], a[1] + part[0])
                total = total + turn(mid, dz - part[2])
            return None, None, HOP**2 * ways, HOP**2 * total
        if dist == 1:
            if dz != 0:
                across = inside_row(a[0] - 1) + inside_row(a[0] + 1) + inside_plane(a[1] - 1) + inside_plane(a[1] + 1)
                along = inside_z(-2 * dz) + inside_z(dz)
            else:
                across = inside_z(1) + inside_z(-1)
                if dy != 0:
                    across = across + inside_plane(a[1] - 1) + inside_plane(a[1] + 1)
                    along = inside_row(a[0] - dy) + inside_row(b[0] + dy)
                else:
                    across = across + inside_row(a[0] - 1) + inside_row(a[0] + 1)
                    along = inside_plane(a[1] - dx) + inside_plane(b[1] + dx)
            walks = (3.0 * across + along + 1.0) * ones
            return None, -HOP, -HOP * (vp + vq), -HOP * (vp * vp + vp * vq + vq * vq) - HOP**3 * walks
        if a[1] == 4:
            return None, None, None, HOP**2 * potential(a[0], 3)
        around = [(a[0] - 1, a[1]), (a[0] + 1, a[1]), (a[0], a[1] - 1), (a[0], a[1] + 1)]
        degree = inside_z(1) + inside_z(-1)
        near = inside_z(-1) * turn(vp, 1) + inside_z(1) * turn(vp, -1)
        for row, plane in around:
            here = inside_row(row) * inside_plane(plane)
            degree = degree + here
            if plane >= 0:
                near = near + here * potential(row, plane)
        square = vp * vp
        return 1.0, vp, square + HOP**2 * degree, vp * square + HOP**2 * (2.0 * degree * vp + near)

    def coefficient(a, b, dz, left):
        right = orbital(b)
        total = None
        for m, h in enumerate(powers(a, b, dz)):
            if h is None:
                continue
            both = left[m] * right
            term = (both[:8] + both[8:]) * h
            total = term if total is None else total + term
        for s in (4, 2, 1):
            total = total + pltpu.roll(total, s, 0)
        if a == b and dz == 0:
            total = total * 0.5
        if dz != 0:
            total = total * inside_z(-dz)
        return total

    if stage == 0:
        gram = jnp.zeros((128, 128), jnp.float32)
        rows = lax.broadcasted_iota(jnp.int32, (128, 128), 0)
        pick_ref[0][...] = (args[1][...] == rows).astype(jnp.float32)
    else:
        gram = args[1][...]
    lefts, sides = [], []
    for a, rights in pairs().items():
        response = None
        for dz in range(-3, 4):
            todo = []
            for b in rights:
                dist = abs(a[0] - b[0]) + abs(a[1] - b[1]) + abs(dz)
                if dist > 3 or stage_of(where, a, b, dz) != stage:
                    continue
                if a != b or dz == 0 or (dz > 0 and a[1] < 4):
                    todo.append((b, dist))
            if not todo:
                continue
            moved = turn(orbital(a), dz)
            least = min(dist for _, dist in todo)
            left = [moved * amp[m] if m >= least else None for m in range(4)]
            acc = None
            for b, _ in todo:
                term = coefficient(a, b, dz, left)[None] * trial(b)
                acc = term if acc is None else acc + term
            acc = turn(acc.reshape(128, 128), -dz)
            response = acc if response is None else response + acc
        if response is None:
            continue
        high, low = halves(trial(a).reshape(128, 128))
        other, rest = halves(response)
        lefts += [high, high, low]
        sides += [other, rest, other]
        if len(lefts) == 6:
            gram = gram + product(lefts, sides, 1, 1)
            lefts, sides = [], []
    if lefts:
        gram = gram + product(lefts, sides, 1, 1)

    if stage < 2:
        out_ref[...] = gram
        return
    gram = (gram + gram.T) * (1.0 / math.sqrt(32 * 64 * 128 * 16))
    pick = args[2][...].astype(jnp.bfloat16)
    gram = product(thirds(gram), [pick] * 3, 1, 0)
    gram = product([pick] * 3, thirds(gram), 0, 0)
    for n in range(2):
        out_ref[pl.ds(n, 128, stride=2), :] = gram


def device(block, slab):
    return ((block % 16) * 8 + slab) * 2 + half_of(slab, block // 16)


def shift_perm(step, dslab):
    return [
        (device(block + step, slab + dslab), device(block, slab))
        for block in range(32)
        for slab in range(8)
        if 0 <= block + step < 32 and slab + dslab < 8
    ]


def local(orbitals, energies, potential, trials, cheb, shifts, column_order):
    smem = pl.BlockSpec(memory_space=pltpu.SMEM)
    vmem = pl.BlockSpec(memory_space=pltpu.VMEM)
    params = pltpu.CompilerParams(vmem_limit_bytes=32 * 1024 * 1024)

    def shape(rows, lead=(16,)):
        return jax.ShapeDtypeStruct((*lead, rows, 128), jnp.float32)

    send, scalars = pl.pallas_call(
        pack_kernel,
        out_shape=[shape(16 * SENT, ()), shape(8, ())],
        in_specs=[smem] * 3 + [pl.BlockSpec(memory_space=pltpu.HBM)] * 3,
        out_specs=[vmem] * 2,
        scratch_shapes=[
            pltpu.VMEM((1024, 128), jnp.float32),
            pltpu.VMEM((128, 128), jnp.float32),
            pltpu.VMEM((256, 128), jnp.float32),
            pltpu.SemaphoreType.DMA((3,)),
        ],
        compiler_params=pltpu.CompilerParams(vmem_limit_bytes=60 * 1024 * 1024),
    )(energies, cheb, shifts, trials.reshape(32, 64, 128), orbitals[0], potential)
    raw = lax.all_to_all(send.reshape(16 * SENT, 1, 128), "trial", split_axis=0, concat_axis=0, tiled=True)

    theirs = lax.ppermute(scalars, "freq", [(0, 1), (1, 0)])

    ahead, above, below, theirs, own = pl.pallas_call(
        halo_kernel,
        out_shape=[shape(len(PARTS[name][0]) * 8 + 8) for name in ("ahead", "above", "below")]
        + [shape(8, ()), shape(len(TILES) * 8)],
        in_specs=[vmem] * 3,
        out_specs=[vmem] * 5,
        compiler_params=params,
    )(raw.reshape(16 * SENT, 128), scalars, theirs)
    ahead = lax.ppermute(ahead, AXES, shift_perm(0, 1))
    above = lax.ppermute(above, AXES, shift_perm(1, 0))
    below = lax.ppermute(below, AXES, shift_perm(-1, 0))

    arrays = {"own": own, "ahead": ahead, "above": above, "below": below}
    partial = pick = None
    for stage, names in enumerate(STAGES):
        operands = [theirs, column_order[None] if stage == 0 else partial]
        if stage == 2:
            operands.append(pick)
        operands += [arrays[name] for name in names]
        shapes = [shape(256 if stage == 2 else 128, ())]
        if stage == 0:
            shapes.append(shape(128, ()))
        partial, *rest = pl.pallas_call(
            functools.partial(kernel, stage),
            out_shape=shapes,
            in_specs=[vmem] * len(operands),
            out_specs=[vmem] * len(shapes),
            compiler_params=params,
            cost_estimate=pl.CostEstimate(flops=2 * 10**9, bytes_accessed=3 * 2**20, transcendentals=0),
        )(*operands)
        pick = rest[0] if rest else pick
    terms = lax.all_to_all(partial, AXES, split_axis=0, concat_axis=0, tiled=True)
    return jnp.sum(terms, axis=0, keepdims=True)


def solution(mesh):
    in_specs = (
        P("trial", "slab", None, None),
        P("trial"),
        P("slab", None, None),
        P("trial", "slab", None, None),
        P("freq", None),
        P("freq"),
        P(),
    )
    out_specs = P(("trial", "slab"), None)
    return jax.shard_map(local, mesh=mesh, in_specs=in_specs, out_specs=out_specs, check_vma=False)
```

```python
import functools
import math

import jax
import jax.numpy as jnp
from jax import lax
from jax.experimental import pallas as pl
from jax.experimental.pallas import tpu as pltpu
from jax.sharding import PartitionSpec as P

AXES = ("trial", "slab", "freq")
HOP = 1.0 / 9.0

TILES = [(0, 0), (0, 1), (0, 2), (0, 3), (1, 0), (1, 1), (1, 2), (1, 3), "o", "e"]
ORB = TILES.index("o") * 8
EXTRA = TILES.index("e") * 8
SENT = EXTRA + 2
OWN = [(row, plane) for row in range(2) for plane in range(4)]
PARTS = {
    "ahead": ([(row, plane) for row in range(2) for plane in range(3)], 0, 4),
    "above": ([(0, 0), (0, 1), (0, 2), (0, 3), (1, 0), (1, 1), (1, 3)], 2, 0),
    "below": ([(1, 0), (1, 1), (1, 2), (1, 3), (0, 2), (0, 3)], -2, 0),
}
AHEAD = PARTS["ahead"][0]


def pieces():
    table = {}
    for rp in OWN:
        table[rp] = ("own", TILES.index(rp) * 8, ORB + OWN.index(rp))
    for name, (taken, drow, dplane) in PARTS.items():
        for k, rp in enumerate(taken):
            orb = k if name == "ahead" else OWN.index(rp)
            table[(rp[0] + drow, rp[1] + dplane)] = (name, k * 8, len(taken) * 8 + orb)
    return table


def pairs():
    ahead = [(row, plane + 4) for row, plane in AHEAD]
    table = {}

    def near(a, b):
        return abs(a[0] - b[0]) + abs(a[1] - b[1]) <= 3

    def add(a, b):
        if near(a, b):
            table.setdefault(a, []).append(b)

    for n, a in enumerate(OWN):
        table.setdefault(a, []).append(a)
        for b in OWN[n + 1 :]:
            add(a, b)
        for b in ahead:
            add(a, b)
        for plane in range(4):
            add(a, (2, plane))
        if a[0] == 1:
            for plane in range(4):
                add(a, (-1, plane))
        if a in ((0, 0), (0, 1), (0, 3)):
            add(a, (3, a[1]))
        if a == (1, 2):
            add(a, (-2, 2))
    for a in ahead:
        if a[1] == 4:
            add(a, a)
        if a[0] == 0:
            others = [(-1, plane) for plane in range(4)] + [(2, 3), (-2, 3)]
        else:
            others = [(2, plane) for plane in range(4)] + [(-1, 3), (3, 3)]
        for b in others:
            add(a, b)
    for plane in range(4):
        add((-1, plane), (2, plane))
    return table


def half_of(slab, freq):
    return freq ^ (((slab + 1) // 2) & 1)


def pack_kernel(energy, cheb, shift, trials_hbm, orbital_hbm, potential_hbm, out_ref, scalars_ref, trials, orbital, potential, sems):
    trial, slab, freq = (lax.axis_index(a) for a in AXES)
    half = freq ^ (lax.div(slab + 1, 2) & 1)
    rows = pl.ds(pl.multiple_of(half * 32, 32), 32)
    copies = [
        pltpu.make_async_copy(source, target, sems.at[n])
        for n, (source, target) in enumerate(
            [
                (trials_hbm.at[:, rows, :], trials.reshape(32, 32, 128)),
                (orbital_hbm.at[:, rows, :], orbital.reshape(4, 32, 128)),
                (potential_hbm, potential.reshape(4, 64, 128)),
            ]
        )
    ]
    for copy in copies:
        copy.start()
    row_of = lax.broadcasted_iota(jnp.int32, (8, 128), 0)
    scalars = jnp.where(row_of == 0, energy[0], 0.0)
    for n, value in enumerate([cheb[0, 0], cheb[0, 1], cheb[0, 2], cheb[0, 3], shift[0]]):
        scalars = jnp.where(row_of == n + 2, value, scalars)
    scalars_ref[...] = scalars
    for copy in copies:
        copy.wait()
    for t in range(16):
        base = t * SENT
        for k, tile in enumerate(TILES):
            if tile == "o":
                for row in range(2):
                    out_ref[base + k * 8 + 4 * row : base + k * 8 + 4 * row + 4, :] = orbital[
                        pl.ds(2 * t + row, 4, stride=32), :
                    ]
            elif tile == "e":
                y = jnp.clip(half * 32 + 2 * t + lax.rem(trial, 4) - 1, 0, 63)
                at = potential[pl.ds(lax.div(trial, 4) * 64 + y, 1), :]
                out_ref[base + k * 8 : base + k * 8 + 2, :] = jnp.where(row_of == 1, at, scalars)[:2]
            else:
                out_ref[base + k * 8 : base + k * 8 + 8, :] = trials[
                    pl.ds(tile[1] * 32 + 2 * t + tile[0], 8, stride=128), :
                ]


def halo_kernel(raw, ours, theirs, ahead, above, below, theirs_ref, own):
    theirs_ref[...] = theirs[...]
    for s in range(16):
        for first in range(0, SENT, 8):
            size = min(8, SENT - first)
            own[s, first : first + size, :] = raw[s * SENT + first : s * SENT + first + size, :]
        own[s, SENT:, :] = ours[2:, :]
    for name, ref in (("ahead", ahead), ("above", above), ("below", below)):
        taken = PARTS[name][0]
        for k, rp in enumerate(taken):
            start = TILES.index(rp) * 8
            ref[:, k * 8 : k * 8 + 8, :] = own[:, start : start + 8, :]
        if name != "ahead":
            ref[:, len(taken) * 8 :, :] = own[:, ORB : ORB + 8, :]
    last = [ORB + OWN.index(rp) for rp in AHEAD] + [EXTRA + 1, EXTRA + 1]
    for k, row in enumerate(last):
        ahead[:, 48 + k : 49 + k, :] = own[:, row : row + 1, :]


STAGES = (("own",), ("own", "ahead"), ("own", "ahead", "above", "below"))


def stage_of(where, a, b, dz):
    names = {where[a][0], where[b][0]}
    if a == b and dz == 0 and a[1] == 3:
        names.add("ahead")
    return next(n for n, held in enumerate(STAGES) if names <= set(held))


def halves(x):
    high = x.astype(jnp.bfloat16)
    return high, (x - high.astype(jnp.float32)).astype(jnp.bfloat16)


def product(lefts, rights, left_dim, right_dim):
    return lax.dot_general(
        jnp.concatenate(lefts, axis=left_dim), jnp.concatenate(rights, axis=right_dim),
        (((left_dim,), (right_dim,)), ((), ())), preferred_element_type=jnp.float32,
    )


def kernel(stage, *args):
    count = 2 if stage == 0 else 1
    out_ref, *pick_ref = args[-count:]
    args = args[:-count]
    refs = dict(zip(STAGES[stage], args[-len(STAGES[stage]) :]))
    own, ahead, theirs = refs["own"], refs.get("ahead"), args[0]
    where = pieces()
    lane = lax.broadcasted_iota(jnp.int32, (8, 128), 1)
    trial_index, slab, freq = (lax.axis_index(a) for a in AXES)
    block = (freq ^ (lax.div(slab + 1, 2) & 1)) * 16 + trial_index

    energy = own[:, EXTRA, :]
    a0 = a1 = a2 = a3 = jnp.zeros((16, 128), jnp.float32)
    for ref, first in ((own.at[0], EXTRA + 2), (theirs, 2)):
        k0, k1, k2, k3, shift = [ref[first + n : first + n + 1, :] for n in range(5)]
        c = (energy + shift) / 4.5
        b0, b1, b2, b3 = k0 - k2, k1 - 3.0 * k3, 2.0 * k2, 4.0 * k3
        a3 = a3 + b3
        a2 = a2 + (b2 - 3.0 * c * b3)
        a1 = a1 + (b1 - 2.0 * c * b2 + 3.0 * c * c * b3)
        a0 = a0 + (b0 - c * b1 + c * c * b2 - c * c * c * b3)
    amp = [a0, a1, a2, a3]

    orb = {}

    def orbital(rp):
        if rp not in orb:
            name, _, row = where[rp]
            orb[rp] = refs[name][:, row, :]
        return orb[rp]

    def trial(rp):
        name, row, _ = where[rp]
        return refs[name][:, row : row + 8, :]

    def turn(x, dz):
        return x if dz == 0 else pltpu.roll(x, dz % 128, x.ndim - 1)

    def inside_row(row):
        y = block * 2 + row
        return ((y >= 0) & (y < 64)).astype(jnp.float32)

    def inside_plane(plane):
        x = slab * 4 + plane
        return ((x >= 0) & (x < 32)).astype(jnp.float32)

    def inside_z(dz):
        return ((lane + dz >= 0) & (lane + dz < 128)).astype(jnp.float32)

    pot = {}

    def potential(row, plane):
        if (row, plane) not in pot:
            ref, at = (own, EXTRA + 1) if plane < 4 else (ahead, 54)
            source = plane % 4 * 4 + row + 1
            pot[(row, plane)] = jnp.broadcast_to(ref[source, at : at + 1, :] / 4.5, (8, 128))
        return pot[(row, plane)]

    ones = jnp.ones((8, 128), jnp.float32)

    def powers(a, b, dz):
        dy, dx = b[0] - a[0], b[1] - a[1]
        step = (dx, dy, dz)
        dist = abs(dx) + abs(dy) + abs(dz)
        ways = math.factorial(dist)
        for s in step:
            ways //= math.factorial(abs(s))
        if dist == 3:
            return None, None, None, -(HOP**3) * ways
        vq = potential(*b) if dist < 3 else None
        vp = turn(potential(*a), dz)
        if dist == 2:
            total = float(ways) * (vp + vq)
            moves = [n for n in range(3) if step[n] != 0]
            for n in moves:
                part = [0, 0, 0]
                part[n] = 1 if step[n] > 0 else -1
                mid = potential(a[0] + part[1], a[1] + part[0])
                total = total + turn(mid, dz - part[2])
            return None, None, HOP**2 * ways, HOP**2 * total
        if dist == 1:
            if dz != 0:
                across = inside_row(a[0] - 1) + inside_row(a[0] + 1) + inside_plane(a[1] - 1) + inside_plane(a[1] + 1)
                along = inside_z(-2 * dz) + inside_z(dz)
            else:
                across = inside_z(1) + inside_z(-1)
                if dy != 0:
                    across = across + inside_plane(a[1] - 1) + inside_plane(a[1] + 1)
                    along = inside_row(a[0] - dy) + inside_row(b[0] + dy)
                else:
                    across = across + inside_row(a[0] - 1) + inside_row(a[0] + 1)
                    along = inside_plane(a[1] - dx) + inside_plane(b[1] + dx)
            walks = (3.0 * across + along + 1.0) * ones
            return None, -HOP, -HOP * (vp + vq), -HOP * (vp * vp + vp * vq + vq * vq) - HOP**3 * walks
        if a[1] == 4:
            return None, None, None, HOP**2 * potential(a[0], 3)
        around = [(a[0] - 1, a[1]), (a[0] + 1, a[1]), (a[0], a[1] - 1), (a[0], a[1] + 1)]
        degree = inside_z(1) + inside_z(-1)
        near = inside_z(-1) * turn(vp, 1) + inside_z(1) * turn(vp, -1)
        for row, plane in around:
            here = inside_row(row) * inside_plane(plane)
            degree = degree + here
            if plane >= 0:
                near = near + here * potential(row, plane)
        square = vp * vp
        return 1.0, vp, square + HOP**2 * degree, vp * square + HOP**2 * (2.0 * degree * vp + near)

    def coefficient(a, b, dz, left):
        right = orbital(b)
        total = None
        for m, h in enumerate(powers(a, b, dz)):
            if h is None:
                continue
            both = left[m] * right
            term = (both[:8] + both[8:]) * h
            total = term if total is None else total + term
        for s in (4, 2, 1):
            total = total + pltpu.roll(total, s, 0)
        if a == b and dz == 0:
            total = total * 0.5
        if dz != 0:
            total = total * inside_z(-dz)
        return total

    if stage == 0:
        gram = jnp.zeros((128, 128), jnp.float32)
        rows = lax.broadcasted_iota(jnp.int32, (128, 128), 0)
        pick_ref[0][...] = (args[1][...] == rows).astype(jnp.float32)
    else:
        gram = args[1][...]
    lefts, sides = [], []
    for a, rights in pairs().items():
        response = None
        for dz in range(-3, 4):
            todo = []
            for b in rights:
                dist = abs(a[0] - b[0]) + abs(a[1] - b[1]) + abs(dz)
                if dist > 3 or stage_of(where, a, b, dz) != stage:
                    continue
                if a != b or dz == 0 or (dz > 0 and a[1] < 4):
                    todo.append((b, dist))
            if not todo:
                continue
            moved = turn(orbital(a), dz)
            least = min(dist for _, dist in todo)
            left = [moved * amp[m] if m >= least else None for m in range(4)]
            acc = None
            for b, _ in todo:
                term = coefficient(a, b, dz, left)[None] * trial(b)
                acc = term if acc is None else acc + term
            acc = turn(acc.reshape(128, 128), -dz)
            response = acc if response is None else response + acc
        if response is None:
            continue
        high, low = halves(trial(a).reshape(128, 128))
        other, rest = halves(response)
        lefts += [high, high, low]
        sides += [other, rest, other]
        if len(lefts) == 6:
            gram = gram + product(lefts, sides, 1, 1)
            lefts, sides = [], []
    if lefts:
        gram = gram + product(lefts, sides, 1, 1)

    if stage < 2:
        out_ref[...] = gram
        return
    gram = (gram + gram.T) * (1.0 / math.sqrt(32 * 64 * 128 * 16))
    pick = args[2][...].astype(jnp.bfloat16)
    gram = product(halves(gram), [pick] * 2, 1, 0)
    gram = product([pick] * 2, halves(gram), 0, 0)
    for n in range(2):
        out_ref[pl.ds(n, 128, stride=2), :] = gram


def device(block, slab):
    return ((block % 16) * 8 + slab) * 2 + half_of(slab, block // 16)


def shift_perm(step, dslab):
    return [
        (device(block + step, slab + dslab), device(block, slab))
        for block in range(32)
        for slab in range(8)
        if 0 <= block + step < 32 and slab + dslab < 8
    ]


def local(orbitals, energies, potential, trials, cheb, shifts, column_order):
    smem = pl.BlockSpec(memory_space=pltpu.SMEM)
    vmem = pl.BlockSpec(memory_space=pltpu.VMEM)
    params = pltpu.CompilerParams(vmem_limit_bytes=32 * 1024 * 1024)

    def shape(rows, lead=(16,)):
        return jax.ShapeDtypeStruct((*lead, rows, 128), jnp.float32)

    send, scalars = pl.pallas_call(
        pack_kernel,
        out_shape=[shape(16 * SENT, ()), shape(8, ())],
        in_specs=[smem] * 3 + [pl.BlockSpec(memory_space=pltpu.HBM)] * 3,
        out_specs=[vmem] * 2,
        scratch_shapes=[
            pltpu.VMEM((1024, 128), jnp.float32),
            pltpu.VMEM((128, 128), jnp.float32),
            pltpu.VMEM((256, 128), jnp.float32),
            pltpu.SemaphoreType.DMA((3,)),
        ],
        compiler_params=pltpu.CompilerParams(vmem_limit_bytes=60 * 1024 * 1024),
    )(energies, cheb, shifts, trials.reshape(32, 64, 128), orbitals[0], potential)
    raw = lax.all_to_all(send.reshape(16 * SENT, 1, 128), "trial", split_axis=0, concat_axis=0, tiled=True)

    theirs = lax.ppermute(scalars, "freq", [(0, 1), (1, 0)])

    ahead, above, below, theirs, own = pl.pallas_call(
        halo_kernel,
        out_shape=[shape(len(PARTS[name][0]) * 8 + 8) for name in ("ahead", "above", "below")]
        + [shape(8, ()), shape(len(TILES) * 8)],
        in_specs=[vmem] * 3,
        out_specs=[vmem] * 5,
        compiler_params=params,
    )(raw.reshape(16 * SENT, 128), scalars, theirs)
    ahead = lax.ppermute(ahead, AXES, shift_perm(0, 1))
    above = lax.ppermute(above, AXES, shift_perm(1, 0))
    below = lax.ppermute(below, AXES, shift_perm(-1, 0))

    arrays = {"own": own, "ahead": ahead, "above": above, "below": below}
    partial = pick = None
    for stage, names in enumerate(STAGES):
        operands = [theirs, column_order[None] if stage == 0 else partial]
        if stage == 2:
            operands.append(pick)
        operands += [arrays[name] for name in names]
        shapes = [shape(256 if stage == 2 else 128, ())]
        if stage == 0:
            shapes.append(shape(128, ()))
        partial, *rest = pl.pallas_call(
            functools.partial(kernel, stage),
            out_shape=shapes,
            in_specs=[vmem] * len(operands),
            out_specs=[vmem] * len(shapes),
            compiler_params=params,
            cost_estimate=pl.CostEstimate(flops=2 * 10**9, bytes_accessed=3 * 2**20, transcendentals=0),
        )(*operands)
        pick = rest[0] if rest else pick
    terms = lax.all_to_all(partial, AXES, split_axis=0, concat_axis=0, tiled=True)
    return jnp.sum(terms, axis=0, keepdims=True)


def solution(mesh):
    in_specs = (
        P("trial", "slab", None, None),
        P("trial"),
        P("slab", None, None),
        P("trial", "slab", None, None),
        P("freq", None),
        P("freq"),
        P(),
    )
    out_specs = P(("trial", "slab"), None)
    return jax.shard_map(local, mesh=mesh, in_specs=in_specs, out_specs=out_specs, check_vma=False)
```

```python
import functools
import math

import jax
import jax.numpy as jnp
from jax import lax
from jax.experimental import pallas as pl
from jax.experimental.pallas import tpu as pltpu
from jax.sharding import PartitionSpec as P

AXES = ("trial", "slab", "freq")
HOP = 1.0 / 9.0

TILES = [(0, 0), (0, 1), (0, 2), (0, 3), (1, 0), (1, 1), (1, 2), (1, 3), "o", "e"]
ORB = TILES.index("o") * 8
EXTRA = TILES.index("e") * 8
SENT = EXTRA + 2
OWN = [(row, plane) for row in range(2) for plane in range(4)]
PARTS = {
    "ahead": ([(row, plane) for row in range(2) for plane in range(3)], 0, 4),
    "above": ([(0, 0), (0, 1), (0, 2), (0, 3), (1, 1), (1, 3)], 2, 0),
    "below": ([(1, 0), (1, 1), (1, 2), (1, 3), (0, 0), (0, 2), (0, 3)], -2, 0),
}
AHEAD = PARTS["ahead"][0]


def pieces():
    table = {}
    for rp in OWN:
        table[rp] = ("own", TILES.index(rp) * 8, ORB + OWN.index(rp))
    for name, (taken, drow, dplane) in PARTS.items():
        for k, rp in enumerate(taken):
            orb = k if name == "ahead" else OWN.index(rp)
            table[(rp[0] + drow, rp[1] + dplane)] = (name, k * 8, len(taken) * 8 + orb)
    return table


def pairs():
    ahead = [(row, plane + 4) for row, plane in AHEAD]
    table = {}

    def near(a, b):
        return abs(a[0] - b[0]) + abs(a[1] - b[1]) <= 3

    def add(a, b):
        if near(a, b):
            table.setdefault(a, []).append(b)

    for n, a in enumerate(OWN):
        table.setdefault(a, []).append(a)
        for b in OWN[n + 1 :]:
            add(a, b)
        for b in ahead:
            add(a, b)
        for plane in range(4):
            add(a, (2, plane))
        if a[0] == 1:
            for plane in range(4):
                add(a, (-1, plane))
        if a in ((0, 1), (0, 3)):
            add(a, (3, a[1]))
        if a in ((1, 0), (1, 2)):
            add(a, (-2, a[1]))
    for a in ahead:
        if a[1] == 4:
            add(a, a)
        if a[0] == 0:
            others = [(-1, plane) for plane in range(4)] + [(2, 3), (-2, 3)]
        else:
            others = [(2, plane) for plane in range(4)] + [(-1, 3), (3, 3)]
        for b in others:
            add(a, b)
    for plane in range(4):
        add((-1, plane), (2, plane))
    return table


def half_of(slab, freq):
    return freq ^ (((slab + 1) // 2) & 1)


def pack_kernel(energy, cheb, shift, trials_hbm, orbital_hbm, potential_hbm, out_ref, scalars_ref, trials, orbital, potential, sems):
    trial, slab, freq = (lax.axis_index(a) for a in AXES)
    half = freq ^ (lax.div(slab + 1, 2) & 1)
    rows = pl.ds(pl.multiple_of(half * 32, 32), 32)
    copies = [
        pltpu.make_async_copy(source, target, sems.at[n])
        for n, (source, target) in enumerate(
            [
                (trials_hbm.at[:, rows, :], trials.reshape(32, 32, 128)),
                (orbital_hbm.at[:, rows, :], orbital.reshape(4, 32, 128)),
                (potential_hbm, potential.reshape(4, 64, 128)),
            ]
        )
    ]
    for copy in copies:
        copy.start()
    row_of = lax.broadcasted_iota(jnp.int32, (8, 128), 0)
    scalars = jnp.where(row_of == 0, energy[0], 0.0)
    for n, value in enumerate([cheb[0, 0], cheb[0, 1], cheb[0, 2], cheb[0, 3], shift[0]]):
        scalars = jnp.where(row_of == n + 2, value, scalars)
    scalars_ref[...] = scalars
    for copy in copies:
        copy.wait()
    for t in range(16):
        base = t * SENT
        for k, tile in enumerate(TILES):
            if tile == "o":
                for row in range(2):
                    out_ref[base + k * 8 + 4 * row : base + k * 8 + 4 * row + 4, :] = orbital[
                        pl.ds(2 * t + row, 4, stride=32), :
                    ]
            elif tile == "e":
                y = jnp.clip(half * 32 + 2 * t + lax.rem(trial, 4) - 1, 0, 63)
                at = potential[pl.ds(lax.div(trial, 4) * 64 + y, 1), :]
                out_ref[base + k * 8 : base + k * 8 + 2, :] = jnp.where(row_of == 1, at, scalars)[:2]
            else:
                out_ref[base + k * 8 : base + k * 8 + 8, :] = trials[
                    pl.ds(tile[1] * 32 + 2 * t + tile[0], 8, stride=128), :
                ]


def halo_kernel(raw, ours, theirs, ahead, above, below, theirs_ref, own):
    theirs_ref[...] = theirs[...]
    for s in range(16):
        for first in range(0, SENT, 8):
            size = min(8, SENT - first)
            own[s, first : first + size, :] = raw[s * SENT + first : s * SENT + first + size, :]
        own[s, SENT:, :] = ours[2:, :]
    for name, ref in (("ahead", ahead), ("above", above), ("below", below)):
        taken = PARTS[name][0]
        for k, rp in enumerate(taken):
            start = TILES.index(rp) * 8
            ref[:, k * 8 : k * 8 + 8, :] = own[:, start : start + 8, :]
        if name != "ahead":
            ref[:, len(taken) * 8 :, :] = own[:, ORB : ORB + 8, :]
    last = [ORB + OWN.index(rp) for rp in AHEAD] + [EXTRA + 1, EXTRA + 1]
    for k, row in enumerate(last):
        ahead[:, 48 + k : 49 + k, :] = own[:, row : row + 1, :]


STAGES = (("own",), ("own", "ahead"), ("own", "ahead", "above", "below"))


def stage_of(where, a, b, dz):
    names = {where[a][0], where[b][0]}
    if a == b and dz == 0 and a[1] == 3:
        names.add("ahead")
    return next(n for n, held in enumerate(STAGES) if names <= set(held))


def halves(x):
    high = x.astype(jnp.bfloat16)
    return high, (x - high.astype(jnp.float32)).astype(jnp.bfloat16)


def thirds(x):
    high = x.astype(jnp.bfloat16)
    middle, low = halves(x - high.astype(jnp.float32))
    return high, middle, low


def product(lefts, rights, left_dim, right_dim):
    return lax.dot_general(
        jnp.concatenate(lefts, axis=left_dim), jnp.concatenate(rights, axis=right_dim),
        (((left_dim,), (right_dim,)), ((), ())), preferred_element_type=jnp.float32,
    )


def kernel(stage, *args):
    count = 2 if stage == 0 else 1
    out_ref, *pick_ref = args[-count:]
    args = args[:-count]
    refs = dict(zip(STAGES[stage], args[-len(STAGES[stage]) :]))
    own, ahead, theirs = refs["own"], refs.get("ahead"), args[0]
    where = pieces()
    lane = lax.broadcasted_iota(jnp.int32, (8, 128), 1)
    trial_index, slab, freq = (lax.axis_index(a) for a in AXES)
    block = (freq ^ (lax.div(slab + 1, 2) & 1)) * 16 + trial_index

    energy = own[:, EXTRA, :]
    a0 = a1 = a2 = a3 = jnp.zeros((16, 128), jnp.float32)
    for ref, first in ((own.at[0], EXTRA + 2), (theirs, 2)):
        k0, k1, k2, k3, shift = [ref[first + n : first + n + 1, :] for n in range(5)]
        c = (energy + shift) / 4.5
        b0, b1, b2, b3 = k0 - k2, k1 - 3.0 * k3, 2.0 * k2, 4.0 * k3
        a3 = a3 + b3
        a2 = a2 + (b2 - 3.0 * c * b3)
        a1 = a1 + (b1 - 2.0 * c * b2 + 3.0 * c * c * b3)
        a0 = a0 + (b0 - c * b1 + c * c * b2 - c * c * c * b3)
    amp = [a0, a1, a2, a3]

    orb = {}

    def orbital(rp):
        if rp not in orb:
            name, _, row = where[rp]
            orb[rp] = refs[name][:, row, :]
        return orb[rp]

    def trial(rp):
        name, row, _ = where[rp]
        return refs[name][:, row : row + 8, :]

    def turn(x, dz):
        return x if dz == 0 else pltpu.roll(x, dz % 128, x.ndim - 1)

    def inside_row(row):
        y = block * 2 + row
        return ((y >= 0) & (y < 64)).astype(jnp.float32)

    def inside_plane(plane):
        x = slab * 4 + plane
        return ((x >= 0) & (x < 32)).astype(jnp.float32)

    def inside_z(dz):
        return ((lane + dz >= 0) & (lane + dz < 128)).astype(jnp.float32)

    pot = {}

    def potential(row, plane):
        if (row, plane) not in pot:
            ref, at = (own, EXTRA + 1) if plane < 4 else (ahead, 54)
            source = plane % 4 * 4 + row + 1
            pot[(row, plane)] = jnp.broadcast_to(ref[source, at : at + 1, :] / 4.5, (8, 128))
        return pot[(row, plane)]

    ones = jnp.ones((8, 128), jnp.float32)

    def powers(a, b, dz):
        dy, dx = b[0] - a[0], b[1] - a[1]
        step = (dx, dy, dz)
        dist = abs(dx) + abs(dy) + abs(dz)
        ways = math.factorial(dist)
        for s in step:
            ways //= math.factorial(abs(s))
        if dist == 3:
            return None, None, None, -(HOP**3) * ways
        vq = potential(*b) if dist < 3 else None
        vp = turn(potential(*a), dz)
        if dist == 2:
            total = float(ways) * (vp + vq)
            moves = [n for n in range(3) if step[n] != 0]
            for n in moves:
                part = [0, 0, 0]
                part[n] = 1 if step[n] > 0 else -1
                mid = potential(a[0] + part[1], a[1] + part[0])
                total = total + turn(mid, dz - part[2])
            return None, None, HOP**2 * ways, HOP**2 * total
        if dist == 1:
            if dz != 0:
                across = inside_row(a[0] - 1) + inside_row(a[0] + 1) + inside_plane(a[1] - 1) + inside_plane(a[1] + 1)
                along = inside_z(-2 * dz) + inside_z(dz)
            else:
                across = inside_z(1) + inside_z(-1)
                if dy != 0:
                    across = across + inside_plane(a[1] - 1) + inside_plane(a[1] + 1)
                    along = inside_row(a[0] - dy) + inside_row(b[0] + dy)
                else:
                    across = across + inside_row(a[0] - 1) + inside_row(a[0] + 1)
                    along = inside_plane(a[1] - dx) + inside_plane(b[1] + dx)
            walks = (3.0 * across + along + 1.0) * ones
            return None, -HOP, -HOP * (vp + vq), -HOP * (vp * vp + vp * vq + vq * vq) - HOP**3 * walks
        if a[1] == 4:
            return None, None, None, HOP**2 * potential(a[0], 3)
        around = [(a[0] - 1, a[1]), (a[0] + 1, a[1]), (a[0], a[1] - 1), (a[0], a[1] + 1)]
        degree = inside_z(1) + inside_z(-1)
        near = inside_z(-1) * turn(vp, 1) + inside_z(1) * turn(vp, -1)
        for row, plane in around:
            here = inside_row(row) * inside_plane(plane)
            degree = degree + here
            if plane >= 0:
                near = near + here * potential(row, plane)
        square = vp * vp
        return 1.0, vp, square + HOP**2 * degree, vp * square + HOP**2 * (2.0 * degree * vp + near)

    def coefficient(a, b, dz, left):
        right = orbital(b)
        total = None
        for m, h in enumerate(powers(a, b, dz)):
            if h is None:
                continue
            both = left[m] * right
            term = (both[:8] + both[8:]) * h
            total = term if total is None else total + term
        for s in (4, 2, 1):
            total = total + pltpu.roll(total, s, 0)
        if a == b and dz == 0:
            total = total * 0.5
        if dz != 0:
            total = total * inside_z(-dz)
        return total

    if stage == 0:
        gram = jnp.zeros((128, 128), jnp.float32)
        rows = lax.broadcasted_iota(jnp.int32, (128, 128), 0)
        pick_ref[0][...] = (args[1][...] == rows).astype(jnp.float32)
    else:
        gram = args[1][...]
    lefts, sides = [], []
    for a, rights in pairs().items():
        response = None
        for dz in range(-3, 4):
            todo = []
            for b in rights:
                dist = abs(a[0] - b[0]) + abs(a[1] - b[1]) + abs(dz)
                if dist > 3 or stage_of(where, a, b, dz) != stage:
                    continue
                if a != b or dz == 0 or (dz > 0 and a[1] < 4):
                    todo.append((b, dist))
            if not todo:
                continue
            moved = turn(orbital(a), dz)
            least = min(dist for _, dist in todo)
            left = [moved * amp[m] if m >= least else None for m in range(4)]
            acc = None
            for b, _ in todo:
                term = coefficient(a, b, dz, left)[None] * trial(b)
                acc = term if acc is None else acc + term
            acc = turn(acc.reshape(128, 128), -dz)
            response = acc if response is None else response + acc
        if response is None:
            continue
        high, low = halves(trial(a).reshape(128, 128))
        other, rest = halves(response)
        lefts += [high, high, low]
        sides += [other, rest, other]
        if len(lefts) == 6:
            gram = gram + product(lefts, sides, 1, 1)
            lefts, sides = [], []
    if lefts:
        gram = gram + product(lefts, sides, 1, 1)

    if stage < 2:
        out_ref[...] = gram
        return
    gram = (gram + gram.T) * (1.0 / math.sqrt(32 * 64 * 128 * 16))
    pick = args[2][...].astype(jnp.bfloat16)
    gram = product(thirds(gram), [pick] * 3, 1, 0)
    gram = product([pick] * 3, thirds(gram), 0, 0)
    for n in range(2):
        out_ref[pl.ds(n, 128, stride=2), :] = gram


def device(block, slab):
    return ((block % 16) * 8 + slab) * 2 + half_of(slab, block // 16)


def shift_perm(step, dslab):
    return [
        (device(block + step, slab + dslab), device(block, slab))
        for block in range(32)
        for slab in range(8)
        if 0 <= block + step < 32 and slab + dslab < 8
    ]


def local(orbitals, energies, potential, trials, cheb, shifts, column_order):
    smem = pl.BlockSpec(memory_space=pltpu.SMEM)
    vmem = pl.BlockSpec(memory_space=pltpu.VMEM)
    params = pltpu.CompilerParams(vmem_limit_bytes=32 * 1024 * 1024)

    def shape(rows, lead=(16,)):
        return jax.ShapeDtypeStruct((*lead, rows, 128), jnp.float32)

    send, scalars = pl.pallas_call(
        pack_kernel,
        out_shape=[shape(16 * SENT, ()), shape(8, ())],
        in_specs=[smem] * 3 + [pl.BlockSpec(memory_space=pltpu.HBM)] * 3,
        out_specs=[vmem] * 2,
        scratch_shapes=[
            pltpu.VMEM((1024, 128), jnp.float32),
            pltpu.VMEM((128, 128), jnp.float32),
            pltpu.VMEM((256, 128), jnp.float32),
            pltpu.SemaphoreType.DMA((3,)),
        ],
        compiler_params=pltpu.CompilerParams(vmem_limit_bytes=60 * 1024 * 1024),
    )(energies, cheb, shifts, trials.reshape(32, 64, 128), orbitals[0], potential)
    raw = lax.all_to_all(send.reshape(16 * SENT, 1, 128), "trial", split_axis=0, concat_axis=0, tiled=True)

    theirs = lax.ppermute(scalars, "freq", [(0, 1), (1, 0)])

    ahead, above, below, theirs, own = pl.pallas_call(
        halo_kernel,
        out_shape=[shape(len(PARTS[name][0]) * 8 + 8) for name in ("ahead", "above", "below")]
        + [shape(8, ()), shape(len(TILES) * 8)],
        in_specs=[vmem] * 3,
        out_specs=[vmem] * 5,
        compiler_params=params,
    )(raw.reshape(16 * SENT, 128), scalars, theirs)
    ahead = lax.ppermute(ahead, AXES, shift_perm(0, 1))
    above = lax.ppermute(above, AXES, shift_perm(1, 0))
    below = lax.ppermute(below, AXES, shift_perm(-1, 0))

    arrays = {"own": own, "ahead": ahead, "above": above, "below": below}
    partial = pick = None
    for stage, names in enumerate(STAGES):
        operands = [theirs, column_order[None] if stage == 0 else partial]
        if stage == 2:
            operands.append(pick)
        operands += [arrays[name] for name in names]
        shapes = [shape(256 if stage == 2 else 128, ())]
        if stage == 0:
            shapes.append(shape(128, ()))
        partial, *rest = pl.pallas_call(
            functools.partial(kernel, stage),
            out_shape=shapes,
            in_specs=[vmem] * len(operands),
            out_specs=[vmem] * len(shapes),
            compiler_params=params,
            cost_estimate=pl.CostEstimate(flops=2 * 10**9, bytes_accessed=3 * 2**20, transcendentals=0),
        )(*operands)
        pick = rest[0] if rest else pick
    terms = lax.all_to_all(partial, AXES, split_axis=0, concat_axis=0, tiled=True)
    return jnp.sum(terms, axis=0, keepdims=True)


def solution(mesh):
    in_specs = (
        P("trial", "slab", None, None),
        P("trial"),
        P("slab", None, None),
        P("trial", "slab", None, None),
        P("freq", None),
        P("freq"),
        P(),
    )
    out_specs = P(("trial", "slab"), None)
    return jax.shard_map(local, mesh=mesh, in_specs=in_specs, out_specs=out_specs, check_vma=False)
```
